128 devices in a mesh: dp: 4 (over x), ctx: 32 (over z, y, core).
Axes of the slice: x: 4, y: 4, z: 4, core: 2. Of those that a mesh axis runs over, the one named last changes fastest.
Arguments:
- query_act: bfloat16 [4, 4096, 4096], P('dp', 'ctx'), may hold values from -22 to 22
- key_act: bfloat16 [4, 4096, 4096], P('dp', 'ctx'), may hold values from -6 to 6
- value_act: bfloat16 [4, 4096, 4096], P('dp', 'ctx'), may hold values from -6 to 6
- out_grad: bfloat16 [4, 4096, 4096], P('dp', 'ctx'), may hold values from -6 to 6
- filter_weight: float32 [4096, 4096], P('ctx'), may hold values from -36 to 36
- first_moment: float32 [4096, 4096], P('ctx', 'dp'), may hold values from -3 to 3
- second_moment: float32 [4096, 4096], P('ctx', 'dp'), may hold values from 0.05 to 2
Outputs:
- query_grad: bfloat16 [4, 4096, 4096], P('dp', 'ctx')
- key_grad: bfloat16 [4, 4096, 4096], P('dp', 'ctx')
- value_grad: bfloat16 [4, 4096, 4096], P('dp', 'ctx')
- new_filter: float32 [4096, 4096], P('ctx', 'dp')
- new_first: float32 [4096, 4096], P('ctx', 'dp')
- new_second: float32 [4096, 4096], P('ctx', 'dp')
The draws below stay inside these ranges and needn't reach their ends.
All inputs are finite; a program needn't handle non-finite values.
Results may differ from the reference program's by a relative error of at most 0.002.
Values sent between devices are 32-bit elements; how exact they have to be, the bound alone decides.
A program may use at most 128 MiB of HBM per device.

```python
import math
import jax
import jax.numpy as jnp
from jax import lax

CHANNELS = 4096
SEQUENCE_LENGTH = 4096
SEQS = 4


def draw_query_act(key, part):
    key = jax.random.fold_in(key, 11)
    key_noise = jax.random.fold_in(key, 1)
    key_scale = jax.random.fold_in(key, 2)
    random_draws = jax.random.truncated_normal(key_noise, -4.0, 4.0, (SEQS, SEQUENCE_LENGTH, CHANNELS), jnp.float32)
    channel_scale = jnp.exp(jax.random.uniform(key_scale, (CHANNELS,), jnp.float32, math.log(0.3), math.log(3.0)))
    channel_ramp = 0.6 + 1.2 * jnp.arange(CHANNELS, dtype=jnp.float32) / CHANNELS
    return (random_draws * channel_scale * channel_ramp).astype(jnp.bfloat16)


def draw_filter_weight(key, part):
    key = jax.random.fold_in(key, 23)
    key_noise = jax.random.fold_in(key, 1)
    key_rate = jax.random.fold_in(key, 2)
    key_spike_seed = jax.random.fold_in(key, 3)
    log_low = math.log(30.0)
    log_high = math.log(64.0 * SEQUENCE_LENGTH)
    horizon = jnp.exp(jax.random.uniform(key_rate, (CHANNELS,), jnp.float32, log_low, log_high))
    position_offsets = jnp.arange(SEQUENCE_LENGTH, dtype=jnp.int32)
    decay_profile = jnp.exp(-position_offsets.astype(jnp.float32)[:, None] / horizon[None, :])
    spike_location = jax.random.randint(key_spike_seed, (4,), 0, SEQUENCE_LENGTH)
    spike_count = jnp.sum((position_offsets[:, None] >= spike_location[None, :]).astype(jnp.float32), axis=1)
    spike_multiplier = jnp.exp(spike_count * math.log(0.6))[:, None]
    energy = jnp.expm1(-2.0 * SEQUENCE_LENGTH / horizon) / jnp.expm1(-2.0 / horizon)
    peak_height = jnp.minimum(jnp.sqrt(SEQUENCE_LENGTH / energy), 8.0)
    random_draws = jax.random.truncated_normal(key_noise, -4.0, 4.0, (SEQUENCE_LENGTH, CHANNELS), jnp.float32)
    return (random_draws * decay_profile * spike_multiplier * peak_height[None, :]).astype(jnp.float32)


def strengthened(values, stream_key, source, target, parts, factor):
    owner, partner = [(jnp.arange(values.shape[dim]) // (values.shape[dim] // parts)).reshape([-1 if axis == dim else 1 for axis in range(values.ndim)]) for dim in (source, target)]
    chosen = jax.random.permutation(stream_key, parts)[partner]
    strong = (owner == chosen) | (owner == (partner + parts // 2) % parts)
    return jnp.where(strong, factor * values, values)


def shard_levels(stream_key, shape, shards, smallest, largest):
    def one(axis_at, blocks):
        draws = jax.random.uniform(jax.random.fold_in(jax.random.fold_in(stream_key, 6), axis_at), (blocks,), jnp.float32, smallest / len(shards), largest / len(shards))
        return jnp.repeat(jnp.exp(draws), shape[axis_at] // blocks).reshape((-1,) + (1,) * (len(shape) - axis_at - 1))

    factor_of = one(*shards[0])
    for cut in shards[1:]:
        factor_of = factor_of * one(*cut)
    return factor_of


def centred(rng, dims, scale, most, shards=(), held_as=jnp.bfloat16):
    level = shard_levels(rng, dims, shards, -0.22, 0.18) if shards else 1.0
    entries = jax.random.normal(rng, dims, jnp.float32) * scale * level
    return jnp.minimum(jnp.maximum(entries, -most), most).astype(held_as)


def gaussian_with(stream_key, dims, deviation, limit, shards, heavy, kind=jnp.bfloat16):
    entries = deviation * jax.random.normal(stream_key, dims, jnp.float32)
    if shards:
        entries = entries * shard_levels(stream_key, dims, shards, -0.22, 0.18)
    return jnp.clip(strengthened(entries, jax.random.fold_in(stream_key, 3), *heavy), -limit, limit).astype(kind)


def setup_inputs(seed: int = 0) -> dict:
    streams_of = jax.random.split(jax.random.key(seed), 8)
    return {
        "query_act": draw_query_act(jax.random.fold_in(streams_of[7], 71), 0),
        "key_act": centred(streams_of[1], (SEQS, SEQUENCE_LENGTH, CHANNELS), 1.0, 6.0, ((0, 4), (1, 32))),
        "value_act": centred(streams_of[2], (SEQS, SEQUENCE_LENGTH, CHANNELS), 1.0, 6.0, ((0, 4), (1, 32))),
        "out_grad": gaussian_with(streams_of[3], (SEQS, SEQUENCE_LENGTH, CHANNELS), 1.0, 6.0, ((0, 4), (1, 32)), (0, 2, 4, 2.0)),
        "filter_weight": draw_filter_weight(jax.random.fold_in(streams_of[7], 71), 0),
        "first_moment": centred(streams_of[5], (SEQUENCE_LENGTH, CHANNELS), 0.5, 3.0, ((0, 32), (1, 4)), jnp.float32),
        "second_moment": jnp.clip(jnp.exp(math.log(2.0) - 3.6888794 * jax.random.uniform(streams_of[6], (SEQUENCE_LENGTH, CHANNELS), jnp.float32) ** shard_levels(streams_of[6], (SEQUENCE_LENGTH, CHANNELS), ((0, 32), (1, 4)), -0.2, 0.2)), 0.05, 2.0),
    }


beta_first = 0.9
beta_second = 0.95
learn_rate = 0.01
decay_rate = 0.1
adam_epsilon = 1e-08
correct_first = 0.9999734386011124
correct_second = 0.994079470779666

def reference(query_act, key_act, value_act, out_grad, filter_weight, first_moment, second_moment):
    padded = 2 * SEQUENCE_LENGTH
    kernel = filter_weight * SEQUENCE_LENGTH ** (-0.5)
    kernel_spec = jnp.fft.rfft(kernel, n=padded, axis=0)

    def one_sequence(inputs):
        query_row, key_row, value_row, grad_row = inputs
        keys_float = key_row.astype(jnp.float32)
        values_float = value_row.astype(jnp.float32)
        upstream = grad_row.astype(jnp.float32)
        mixed_in = keys_float * values_float
        gated_in = upstream * query_row.astype(jnp.float32)
        mixed_spec = jnp.fft.rfft(mixed_in, n=padded, axis=0)
        gated_spec = jnp.fft.rfft(gated_in, n=padded, axis=0)
        conv_out = jnp.fft.irfft(kernel_spec * mixed_spec, n=padded, axis=0)[:SEQUENCE_LENGTH]
        back_in = jnp.fft.irfft(jnp.conj(kernel_spec) * gated_spec, n=padded, axis=0)[:SEQUENCE_LENGTH]
        lag_part = jnp.fft.irfft(jnp.conj(mixed_spec) * gated_spec, n=padded, axis=0)[:SEQUENCE_LENGTH]
        return ((upstream * conv_out).astype(jnp.bfloat16), (back_in * values_float).astype(jnp.bfloat16), (back_in * keys_float).astype(jnp.bfloat16), lag_part.astype(jnp.float32))
    query_grad, key_grad, value_grad, lag_parts = lax.map(one_sequence, (query_act, key_act, value_act, out_grad))
    lag_grad = lax.optimization_barrier(jnp.sum(lag_parts, axis=0))
    total_sq = jnp.sum(lag_grad * lag_grad)
    bad_count = jnp.sum(jnp.logical_not(jnp.isfinite(lag_grad)).astype(jnp.float32))
    root_mean = jnp.sqrt(total_sq / (SEQUENCE_LENGTH * CHANNELS) + 1e-06)
    clipped = lag_grad * jnp.minimum(1.0, 1.0 / root_mean)
    first_next = beta_first * first_moment + (1.0 - beta_first) * clipped
    second_next = beta_second * second_moment + (1.0 - beta_second) * clipped * clipped
    update = first_next / correct_first / (jnp.sqrt(second_next / correct_second) + adam_epsilon) + decay_rate * filter_weight
    filter_next = filter_weight - learn_rate * update
    commit = bad_count == 0.0
    return (query_grad, key_grad, value_grad, jnp.where(commit, filter_next, filter_weight), jnp.where(commit, first_next, first_moment), jnp.where(commit, second_next, second_moment))
```

```python
import functools
import math

import jax
import jax.numpy as jnp
import numpy as np
from jax import lax
from jax.experimental import pallas as pl
from jax.experimental.pallas import tpu as pltpu
from jax.sharding import PartitionSpec as P

MESH = pl.DeviceIdType.MESH
F32 = jnp.float32
BF16 = jnp.bfloat16

DP = 4
CTX = 32
ROWS = 128
LANES = 128
PERIOD = CTX * ROWS

beta_first = 0.9
beta_second = 0.95
learn_rate = 0.01
decay_rate = 0.1
adam_epsilon = 1e-08
correct_first = 0.9999734386011124
correct_second = 0.994079470779666


def dft_tables():
    k1 = np.arange(CTX)[:, None, None]
    m = np.arange(ROWS)[None, :, None]
    j = np.arange(ROWS)[None, None, :]
    turns = (j * (4 * k1 + 1 + 4 * CTX * m)) % (4 * PERIOD)
    angle = turns * (2.0 * np.pi / (4 * PERIOD))
    cosine, sine = np.cos(angle), np.sin(angle)
    forward = np.concatenate([cosine, sine], axis=2)
    inverse = np.concatenate([cosine.swapaxes(1, 2), sine.swapaxes(1, 2)], axis=2) / PERIOD
    out = []
    for table in (forward, inverse):
        high = table.astype(jnp.bfloat16)
        low = (table - high.astype(np.float64)).astype(jnp.bfloat16)
        out += [high, low]
    return np.stack(out)


def rotated(value, turn):
    re, im = value
    turn = turn % 1.0
    if turn == 0.0:
        return value
    c, s = math.cos(2 * math.pi * turn), math.sin(2 * math.pi * turn)
    return (re * c + im * s, im * c - re * s)


def dft8(v, sign):
    half = math.sqrt(0.5)

    def add(a, b):
        return (a[0] + b[0], a[1] + b[1])

    def sub(a, b):
        return (a[0] - b[0], a[1] - b[1])

    def quarter(a):
        return (a[1], -a[0]) if sign > 0 else (-a[1], a[0])

    def sub_quarter(a, b):
        if sign > 0:
            return (a[0] + b[1], a[1] - b[0]), (a[0] - b[1], a[1] + b[0])
        return (a[0] - b[1], a[1] + b[0]), (a[0] + b[1], a[1] - b[0])

    def dft4(a, b, c, d):
        s0, s1 = add(a, c), sub(a, c)
        s2, s3 = add(b, d), sub(b, d)
        y1, y3 = sub_quarter(s1, s3)
        return add(s0, s2), y1, sub(s0, s2), y3

    e = dft4(v[0], v[2], v[4], v[6])
    o = dft4(v[1], v[3], v[5], v[7])
    if sign > 0:
        o1 = ((o[1][0] + o[1][1]) * half, (o[1][1] - o[1][0]) * half)
        o3 = ((o[3][1] - o[3][0]) * half, (o[3][0] + o[3][1]) * (-half))
    else:
        o1 = ((o[1][0] - o[1][1]) * half, (o[1][1] + o[1][0]) * half)
        o3 = ((o[3][0] + o[3][1]) * (-half), (o[3][0] - o[3][1]) * half)
    y2, y6 = sub_quarter(e[2], o[2])
    return [
        add(e[0], o[0]), add(e[1], o1), y2, add(e[3], o3),
        sub(e[0], o[0]), sub(e[1], o1), y6, sub(e[3], o3),
    ]


def lead_forward(x):
    c1, s1 = math.cos(math.pi / 8), math.sin(math.pi / 8)
    half = math.sqrt(0.5)
    u = [[None] * 8 for _ in range(4)]
    for a0 in range(8):
        x0, x1, x2, x3 = x[a0], x[a0 + 8], x[a0 + 16], x[a0 + 24]
        p1r, p1i = x1 * c1, x1 * s1
        p3r, p3i = x3 * s1, x3 * c1
        s = x2 * half
        ep, em = x0 + s, x0 - s
        sr, si = p1r + p3r, p1i + p3i
        dr, di = p1r - p3r, p1i - p3i
        u[0][a0] = (ep + sr, -(s + si))
        u[2][a0] = (ep - sr, si - s)
        u[1][a0] = (em - di, s - dr)
        u[3][a0] = (em + di, s + dr)
    out = [None] * 32
    for q in range(4):
        y = dft8([rotated(u[q][a0], a0 * (4 * q + 1) / 128.0) for a0 in range(8)], 1)
        for r in range(8):
            out[q + 4 * r] = y[r]
    return out


def lead_inverse(v):
    c1, s1 = math.cos(math.pi / 8), math.sin(math.pi / 8)
    half = math.sqrt(0.5)
    u = []
    for q in range(4):
        t = dft8([v[q + 4 * r] for r in range(8)], -1)
        u.append([rotated(t[a0], -a0 * (4 * q + 1) / 128.0) for a0 in range(8)])
    out = [None] * 32
    for a0 in range(8):
        (r0, i0), (r1, i1), (r2, i2), (r3, i3) = u[0][a0], u[1][a0], u[2][a0], u[3][a0]
        ar, ai, br, bi = r0 + r2, i0 + i2, r0 - r2, i0 - i2
        cr, ci, dr, di = r1 + r3, i1 + i3, r1 - r3, i1 - i3
        out[a0] = ar + cr
        out[a0 + 8] = (br - di) * c1 - (bi + dr) * s1
        out[a0 + 16] = ((ar - cr) - (ai - ci)) * half
        out[a0 + 24] = (br + di) * s1 - (bi - dr) * c1
    return out


def owner_plane(ctx):
    z, y, core = ctx // 8, (ctx // 2) % 4, ctx % 2
    return 2 * ((z + y) % 2) + core


def owner_slot(ctx):
    z, y = ctx // 8, (ctx // 2) % 4
    return 2 * z + y // 2


def channel_block(ctx):
    return owner_plane(ctx) * 8 + owner_slot(ctx)


def summing_level(plane):
    return 2 * (plane % 2) + (1 - plane // 2)


def split(value):
    high = value.astype(BF16)
    return high, (value - high.astype(F32)).astype(BF16)


def times_table(table, kind, k1, re, im):
    wide = jnp.concatenate([re, im], axis=1)
    high, low = split(wide)

    def paired(part):
        other = jnp.concatenate([part[:, LANES:], -part[:, :LANES]], axis=1)
        return jnp.concatenate([part, other], axis=0)

    high, low = paired(high), paired(low)
    t_high, t_low = table[kind, k1], table[kind + 1, k1]
    dot = functools.partial(jnp.dot, preferred_element_type=F32)
    return dot(t_high, high) + dot(t_low, high) + dot(t_high, low)


def body(
    q_hbm, k_hbm, v_hbm, g_hbm, filt_hbm, m1_hbm, m2_hbm, tab_hbm,
    qg_hbm, kg_hbm, vg_hbm, nf_hbm, n1_hbm, n2_hbm,
    q_in, k_in, v_in, g_in, filt_part, filt_own, m1, m2, tab,
    send_m, send_g, send_b, got_m, got_k, got_g, work, spec_k, spec_m, spec_g,
    got_conv, got_back, parts, summed, lag,
    tile_mine, tile_x, tile_row, tile_all,
    load_sem, out_sem, ksend, krecv, kxsend, kxrecv, msend, mrecv, gsend, grecv,
    csend, crecv, bsend, brecv, psend, precv, lsend, lrecv, xsend, xrecv, asend, arecv, own_sem,
):
    d = lax.axis_index("dp")
    c = lax.axis_index("ctx")
    plane = owner_plane(c)
    slot = owner_slot(c)
    mine = channel_block(c)
    z, y = c // 8, (c // 2) % 4

    loads = {}
    def load(name, index, source, target):
        loads[name] = pltpu.make_async_copy(source, target, load_sem.at[index])
        loads[name].start()

    load("filt", 0, filt_hbm.at[pl.ds(pl.multiple_of(d * 32, 32), 32)], filt_part)
    load("k", 1, k_hbm.at[0], k_in)
    load("v", 2, v_hbm.at[0], v_in)
    load("g", 3, g_hbm.at[0], g_in)
    load("q", 4, q_hbm.at[0], q_in)
    load("tab", 5, tab_hbm, tab)
    load("own", 6, filt_hbm.at[:, pl.ds(pl.multiple_of(d * 1024, 1024), 1024)], filt_own)
    load("m1", 7, m1_hbm, m1)
    load("m2", 8, m2_hbm, m2)

    level = (z + y) % 4
    helper = 2 * (1 - level % 2) + level // 2

    def lag_source(h):
        hz = h // 2
        hy = 2 * (h % 2) + (d // 2 + hz) % 2
        return hz * 8 + hy * 2 + d % 2

    def lag_target(i, of_plane):
        tz = i // 2
        ty = (summing_level(of_plane) - tz + 4) % 4
        return tz * 8 + ty * 2 + i % 2

    barrier = pltpu.get_barrier_semaphore()

    def greet(i, carry):
        pl.semaphore_signal(barrier, inc=1, device_id=(d, (c + i) % CTX), device_id_type=MESH)
        return carry

    lax.fori_loop(1, CTX, greet, 0)
    for step in range(1, DP):
        pl.semaphore_signal(barrier, inc=1, device_id=((d + step) % DP, c), device_id_type=MESH)

    def greet_lag(h, carry):
        pl.semaphore_signal(barrier, inc=1, device_id=(helper, lag_source(h)), device_id_type=MESH)
        return carry

    lax.fori_loop(0, 8, greet_lag, 0)
    pl.semaphore_wait(barrier, 31 + 3 + 8)

    def peer(i):
        return (c + i) % CTX

    def wait_bytes(ref, sem):
        pltpu.make_async_copy(ref, ref, sem).wait()

    quarter = pl.ds(pl.multiple_of(d * 32, 32), 32)

    def filt_cols(block):
        return filt_part.at[:, pl.ds(pl.multiple_of(block * LANES, LANES), LANES)]

    loads["filt"].wait()

    def send_filter(i, carry):
        t = peer(i)
        pltpu.make_async_remote_copy(
            src_ref=filt_cols(channel_block(t)), dst_ref=got_k.at[c, quarter],
            send_sem=ksend, recv_sem=krecv, device_id=(d, t), device_id_type=MESH,
        ).start()
        return carry

    lax.fori_loop(1, CTX, send_filter, 0)
    own_copy = pltpu.make_async_copy(filt_cols(mine), got_k.at[c, quarter], own_sem)
    own_copy.start()

    def product_out(left, right, store, target, ssem, rsem):
        def block(i, carry):
            t = peer(i)
            b = channel_block(t)
            cols = pl.ds(pl.multiple_of(b * LANES, LANES), LANES)
            store[b] = left[:, cols].astype(F32) * right[:, cols].astype(F32)
            pltpu.make_async_remote_copy(
                src_ref=store.at[b], dst_ref=target.at[c],
                send_sem=ssem, recv_sem=rsem, device_id=(d, t), device_id_type=MESH,
            ).start()
            return carry

        lax.fori_loop(1, CTX, block, 0)
        cols = pl.ds(pl.multiple_of(mine * LANES, LANES), LANES)
        target[c] = left[:, cols].astype(F32) * right[:, cols].astype(F32)

    loads["k"].wait()
    loads["v"].wait()
    product_out(k_in, v_in, send_m, got_m, msend, mrecv)

    own_copy.wait()
    wait_bytes(got_k.at[pl.ds(0, 31), quarter], krecv)
    share = []
    for step in range(1, DP):
        copy = pltpu.make_async_remote_copy(
            src_ref=got_k.at[:, quarter], dst_ref=got_k.at[:, quarter],
            send_sem=kxsend.at[step - 1], recv_sem=kxrecv.at[step - 1],
            device_id=((d + step) % DP, c), device_id_type=MESH,
        )
        copy.start()
        share.append(copy)

    loads["g"].wait()
    loads["q"].wait()
    product_out(g_in, q_in, send_g, got_g, gsend, grecv)

    def forward(got, spec, scale=None):
        def lead(i, carry):
            rows = pl.ds(pl.multiple_of(i * 8, 8), 8)
            x = [got[a, rows] for a in range(CTX)]
            if scale is not None:
                x = [value * scale for value in x]
            for k1, (re, im) in enumerate(lead_forward(x)):
                work[k1, rows, :LANES] = re
                work[k1, rows, LANES:] = im
            return carry

        lax.fori_loop(0, ROWS // 8, lead, 0)

        def rest(i, carry):
            for k1 in (2 * i, 2 * i + 1):
                spec[k1] = times_table(tab, 0, k1, work[k1, :, :LANES], work[k1, :, LANES:])
            return carry

        lax.fori_loop(0, CTX // 2, rest, 0)

    def inverse(left, right, conjugate, out):
        def rest(i, carry):
            for k1 in (2 * i, 2 * i + 1):
                lr, li = left[k1, :, :LANES], left[k1, :, LANES:]
                rr, ri = right[k1, :, :LANES], right[k1, :, LANES:]
                if conjugate:
                    re, im = lr * rr + li * ri, li * rr - lr * ri
                else:
                    re, im = lr * rr - li * ri, -(lr * ri + li * rr)
                work[k1] = times_table(tab, 2, k1, re, im)
            return carry

        lax.fori_loop(0, CTX // 2, rest, 0)

        def lead(i, carry):
            rows = pl.ds(pl.multiple_of(i * 8, 8), 8)
            v = [(work[k1, rows, :LANES], -work[k1, rows, LANES:]) for k1 in range(CTX)]
            for a, value in enumerate(lead_inverse(v)):
                out[a, rows] = value
            return carry

        lax.fori_loop(0, ROWS // 8, lead, 0)

    def send_back(source, target, ssem, rsem):
        def block(i, carry):
            t = peer(i)
            pltpu.make_async_remote_copy(
                src_ref=source.at[t], dst_ref=target.at[mine],
                send_sem=ssem, recv_sem=rsem, device_id=(d, t), device_id_type=MESH,
            ).start()
            return carry

        lax.fori_loop(1, CTX, block, 0)
        copy = pltpu.make_async_copy(source.at[c], target.at[mine], own_sem)
        copy.start()
        return copy

    blocks = pl.ds(0, CTX - 1)
    loads["tab"].wait()
    wait_bytes(got_m.at[blocks], mrecv)
    forward(got_m, spec_m)
    for copy in share:
        copy.wait()
    forward(got_k, spec_k, PERIOD**-0.5)
    wait_bytes(send_m.at[blocks], msend)
    inverse(spec_k, spec_m, False, send_m)
    conv_own = send_back(send_m, got_conv, csend, crecv)

    wait_bytes(got_g.at[blocks], grecv)
    forward(got_g, spec_g)
    wait_bytes(send_g.at[blocks], gsend)
    inverse(spec_m, spec_g, True, send_g)

    share = []
    for step in range(1, DP):
        to = (d + step) % DP
        for pair in range(4):
            copy = pltpu.make_async_remote_copy(
                src_ref=send_g.at[pl.ds(lag_target(2 * pair, to), 2)],
                dst_ref=parts.at[step - 1, pl.ds(2 * pair, 2)],
                send_sem=psend.at[step - 1, pair], recv_sem=precv.at[step - 1, pair],
                device_id=(to, c), device_id_type=MESH,
            )
            copy.start()
            share.append(copy)

    inverse(spec_k, spec_g, True, send_b)
    conv_own.wait()
    back_own = send_back(send_b, got_back, bsend, brecv)

    wait_bytes(got_conv.at[blocks], crecv)

    def finish_conv(b, carry):
        cols = pl.ds(pl.multiple_of(b * LANES, LANES), LANES)
        q_in[:, cols] = (g_in[:, cols].astype(F32) * got_conv[b]).astype(BF16)
        return carry

    lax.fori_loop(0, CTX, finish_conv, 0)
    outs = []

    def write_out(index, source, target):
        copy = pltpu.make_async_copy(source, target, out_sem.at[index])
        copy.start()
        outs.append(copy)

    write_out(0, q_in, qg_hbm.at[0])

    for copy in share:
        copy.wait()

    def add_up(i, carry):
        t = lag_target(i, d)
        summed[i] = (send_g[t] + parts[0, i]) + (parts[1, i] + parts[2, i])
        pltpu.make_async_remote_copy(
            src_ref=summed.at[i], dst_ref=lag.at[slot],
            send_sem=lsend, recv_sem=lrecv, device_id=(plane, t), device_id_type=MESH,
        ).start()
        return carry

    lax.fori_loop(0, 8, add_up, 0)
    wait_bytes(lag, lrecv)

    def measure(i, carry):
        squares, bad = carry
        value = lag[i].reshape(16, 8, LANES)
        finite = jnp.abs(value) < jnp.inf
        return (
            squares + jnp.sum(value * value, axis=0),
            bad + jnp.sum(jnp.where(finite, 0.0, 1.0), axis=0),
        )

    nothing = jnp.zeros((8, LANES), F32)
    squares, bad = lax.fori_loop(0, 8, measure, (nothing, nothing))
    tile_mine[:8] = squares
    tile_mine[8:] = bad
    share = []
    for step in range(1, DP):
        copy = pltpu.make_async_remote_copy(
            src_ref=tile_mine, dst_ref=tile_x.at[step - 1],
            send_sem=xsend.at[step - 1], recv_sem=xrecv.at[step - 1],
            device_id=((d + step) % DP, c), device_id_type=MESH,
        )
        copy.start()
        share.append(copy)
    for copy in share:
        copy.wait()
    tile_row[...] = (tile_mine[...] + tile_x[0]) + (tile_x[1] + tile_x[2])

    def spread(i, carry):
        pltpu.make_async_remote_copy(
            src_ref=tile_row, dst_ref=tile_all.at[c],
            send_sem=asend, recv_sem=arecv, device_id=(d, peer(i)), device_id_type=MESH,
        ).start()
        return carry

    lax.fori_loop(1, CTX, spread, 0)
    tile_all[c] = tile_row[...]

    back_own.wait()
    wait_bytes(got_back.at[blocks], brecv)

    def finish_back(b, carry):
        cols = pl.ds(pl.multiple_of(b * LANES, LANES), LANES)
        back = got_back[b]
        keys, values = k_in[:, cols].astype(F32), v_in[:, cols].astype(F32)
        v_in[:, cols] = (back * values).astype(BF16)
        k_in[:, cols] = (back * keys).astype(BF16)
        return carry

    lax.fori_loop(0, CTX, finish_back, 0)
    write_out(1, v_in, kg_hbm.at[0])
    write_out(2, k_in, vg_hbm.at[0])

    wait_bytes(tile_all.at[blocks], arecv)
    everything = jnp.sum(tile_all[...], axis=0)
    total_sq = jnp.sum(everything[:8])
    bad_count = jnp.sum(everything[8:])
    mean_sq = jnp.full((8, LANES), total_sq) * (1.0 / (PERIOD * 4096)) + 1e-06
    factor = jnp.minimum(1.0, 1.0 / jnp.sqrt(mean_sq))[:1]
    commit = (jnp.full((8, LANES), bad_count) == 0.0)[:1]
    loads["own"].wait()
    loads["m1"].wait()
    loads["m2"].wait()

    def step(h, carry):
        cols = pl.ds(pl.multiple_of(h * LANES, LANES), LANES)
        clipped = lag[h] * factor
        first, second, weight = m1[:, cols], m2[:, cols], filt_own[:, cols]
        first_next = beta_first * first + (1.0 - beta_first) * clipped
        second_next = beta_second * second + (1.0 - beta_second) * clipped * clipped
        update = (
            first_next / correct_first / (jnp.sqrt(second_next / correct_second) + adam_epsilon)
            + decay_rate * weight
        )
        filt_own[:, cols] = jnp.where(commit, weight - learn_rate * update, weight)
        m1[:, cols] = jnp.where(commit, first_next, first)
        m2[:, cols] = jnp.where(commit, second_next, second)
        return carry

    lax.fori_loop(0, 8, step, 0)
    write_out(3, filt_own, nf_hbm)
    write_out(4, m1, n1_hbm)
    write_out(5, m2, n2_hbm)

    wait_bytes(got_k.at[blocks, quarter], ksend)
    wait_bytes(send_m.at[blocks], csend)
    wait_bytes(send_b.at[blocks], bsend)
    wait_bytes(summed, lsend)
    wait_bytes(tile_all.at[blocks], asend)
    for copy in outs:
        copy.wait()


def on_device(query_act, key_act, value_act, out_grad, filter_weight, first_moment, second_moment):
    table = jnp.asarray(dft_tables())
    block = (CTX, ROWS, LANES)
    wide = (CTX, ROWS, 2 * LANES)
    vmem = pltpu.VMEM
    dma = pltpu.SemaphoreType.DMA
    anywhere = pl.BlockSpec(memory_space=pl.ANY)
    stream = jax.ShapeDtypeStruct(query_act.shape, BF16)
    state = jax.ShapeDtypeStruct(first_moment.shape, F32)
    return pl.pallas_call(
        body,
        out_shape=(stream, stream, stream, state, state, state),
        in_specs=[anywhere] * 8,
        out_specs=(anywhere,) * 6,
        scratch_shapes=[
            vmem((ROWS, 4096), BF16), vmem((ROWS, 4096), BF16),
            vmem((ROWS, 4096), BF16), vmem((ROWS, 4096), BF16),
            vmem((32, 4096), F32), vmem((ROWS, 1024), F32),
            vmem((ROWS, 1024), F32), vmem((ROWS, 1024), F32),
            vmem((4,) + wide, BF16),
            vmem(block, F32), vmem(block, F32), vmem(block, F32),
            vmem(block, F32), vmem(block, F32), vmem(block, F32),
            vmem(wide, F32), vmem(wide, F32), vmem(wide, F32), vmem(wide, F32),
            vmem(block, F32), vmem(block, F32),
            vmem((3, 8, ROWS, LANES), F32), vmem((8, ROWS, LANES), F32), vmem((8, ROWS, LANES), F32),
            vmem((16, LANES), F32), vmem((3, 16, LANES), F32), vmem((16, LANES), F32),
            vmem((CTX, 16, LANES), F32),
            dma((9,)), dma((6,)), dma, dma, dma((3,)), dma((3,)), dma, dma, dma, dma,
            dma, dma, dma, dma, dma((3, 4)), dma((3, 4)), dma, dma, dma((3,)), dma((3,)), dma, dma, dma,
        ],
        compiler_params=pltpu.CompilerParams(
            collective_id=0, has_side_effects=True, vmem_limit_bytes=60 * 2**20
        ),
    )(query_act, key_act, value_act, out_grad, filter_weight, first_moment, second_moment, table)


def solution(mesh):
    return jax.shard_map(
        on_device,
        mesh=mesh,
        in_specs=(
            P("dp", "ctx", None),
            P("dp", "ctx", None),
            P("dp", "ctx", None),
            P("dp", "ctx", None),
            P("ctx", None),
            P("ctx", "dp"),
            P("ctx", "dp"),
        ),
        out_specs=(
            P("dp", "ctx", None),
            P("dp", "ctx", None),
            P("dp", "ctx", None),
            P("ctx", "dp"),
            P("ctx", "dp"),
            P("ctx", "dp"),
        ),
        check_vma=False,
    )
```

```python
import functools
import math

import jax
import jax.numpy as jnp
import numpy as np
from jax import lax
from jax.experimental import pallas as pl
from jax.experimental.pallas import tpu as pltpu
from jax.sharding import PartitionSpec as P

MESH = pl.DeviceIdType.MESH
F32 = jnp.float32
BF16 = jnp.bfloat16

DP = 4
CTX = 32
ROWS = 128
LANES = 128
VMEM_MIB = 60
PERIOD = CTX * ROWS
STEPS = (
    (2, 2), (2, 3), (3, 2), (2, 1), (1, 2), (2, 0), (0, 2), (1, 1),
    (3, 3), (1, 3), (3, 1), (0, 1), (1, 0), (0, 3), (3, 0),
)

beta_first = 0.9
beta_second = 0.95
learn_rate = 0.01
decay_rate = 0.1
adam_epsilon = 1e-08
correct_first = 0.9999734386011124
correct_second = 0.994079470779666


def dft_tables():
    k1 = np.arange(CTX)[:, None, None]
    m = np.arange(ROWS)[None, :, None]
    j = np.arange(ROWS)[None, None, :]
    turns = (j * (4 * k1 + 1 + 4 * CTX * m)) % (4 * PERIOD)
    angle = turns * (2.0 * np.pi / (4 * PERIOD))
    cosine, sine = np.cos(angle), np.sin(angle)
    forward = np.concatenate([cosine, sine], axis=2)
    inverse = np.concatenate([cosine.swapaxes(1, 2), sine.swapaxes(1, 2)], axis=2) / PERIOD
    out = []
    for table in (forward, inverse):
        high = table.astype(jnp.bfloat16)
        low = (table - high.astype(np.float64)).astype(jnp.bfloat16)
        out += [high, low]
    return np.stack(out)


def rotated(value, turn):
    re, im = value
    turn = turn % 1.0
    if turn == 0.0:
        return value
    c, s = math.cos(2 * math.pi * turn), math.sin(2 * math.pi * turn)
    return (re * c + im * s, im * c - re * s)


def dft8(v, sign):
    half = math.sqrt(0.5)

    def add(a, b):
        return (a[0] + b[0], a[1] + b[1])

    def sub(a, b):
        return (a[0] - b[0], a[1] - b[1])

    def quarter(a):
        return (a[1], -a[0]) if sign > 0 else (-a[1], a[0])

    def sub_quarter(a, b):
        if sign > 0:
            return (a[0] + b[1], a[1] - b[0]), (a[0] - b[1], a[1] + b[0])
        return (a[0] - b[1], a[1] + b[0]), (a[0] + b[1], a[1] - b[0])

    def dft4(a, b, c, d):
        s0, s1 = add(a, c), sub(a, c)
        s2, s3 = add(b, d), sub(b, d)
        y1, y3 = sub_quarter(s1, s3)
        return add(s0, s2), y1, sub(s0, s2), y3

    e = dft4(v[0], v[2], v[4], v[6])
    o = dft4(v[1], v[3], v[5], v[7])
    if sign > 0:
        o1 = ((o[1][0] + o[1][1]) * half, (o[1][1] - o[1][0]) * half)
        o3 = ((o[3][1] - o[3][0]) * half, (o[3][0] + o[3][1]) * (-half))
    else:
        o1 = ((o[1][0] - o[1][1]) * half, (o[1][1] + o[1][0]) * half)
        o3 = ((o[3][0] + o[3][1]) * (-half), (o[3][0] - o[3][1]) * half)
    y2, y6 = sub_quarter(e[2], o[2])
    return [
        add(e[0], o[0]), add(e[1], o1), y2, add(e[3], o3),
        sub(e[0], o[0]), sub(e[1], o1), y6, sub(e[3], o3),
    ]


def lead_forward(x):
    c1, s1 = math.cos(math.pi / 8), math.sin(math.pi / 8)
    half = math.sqrt(0.5)
    u = [[None] * 8 for _ in range(4)]
    for a0 in range(8):
        x0, x1, x2, x3 = x[a0], x[a0 + 8], x[a0 + 16], x[a0 + 24]
        p1r, p1i = x1 * c1, x1 * s1
        p3r, p3i = x3 * s1, x3 * c1
        s = x2 * half
        ep, em = x0 + s, x0 - s
        sr, si = p1r + p3r, p1i + p3i
        dr, di = p1r - p3r, p1i - p3i
        u[0][a0] = (ep + sr, -(s + si))
        u[2][a0] = (ep - sr, si - s)
        u[1][a0] = (em - di, s - dr)
        u[3][a0] = (em + di, s + dr)
    out = [None] * 32
    for q in range(4):
        y = dft8([rotated(u[q][a0], a0 * (4 * q + 1) / 128.0) for a0 in range(8)], 1)
        for r in range(8):
            out[q + 4 * r] = y[r]
    return out


def lead_inverse(v):
    c1, s1 = math.cos(math.pi / 8), math.sin(math.pi / 8)
    half = math.sqrt(0.5)
    u = []
    for q in range(4):
        t = dft8([v[q + 4 * r] for r in range(8)], -1)
        u.append([rotated(t[a0], -a0 * (4 * q + 1) / 128.0) for a0 in range(8)])
    out = [None] * 32
    for a0 in range(8):
        (r0, i0), (r1, i1), (r2, i2), (r3, i3) = u[0][a0], u[1][a0], u[2][a0], u[3][a0]
        ar, ai, br, bi = r0 + r2, i0 + i2, r0 - r2, i0 - i2
        cr, ci, dr, di = r1 + r3, i1 + i3, r1 - r3, i1 - i3
        out[a0] = ar + cr
        out[a0 + 8] = (br - di) * c1 - (bi + dr) * s1
        out[a0 + 16] = ((ar - cr) - (ai - ci)) * half
        out[a0 + 24] = (br + di) * s1 - (bi - dr) * c1
    return out


def owner_plane(ctx):
    z, y, core = ctx // 8, (ctx // 2) % 4, ctx % 2
    return 2 * ((z + y) % 2) + core


def owner_slot(ctx):
    z, y = ctx // 8, (ctx // 2) % 4
    return 2 * z + y // 2


def channel_block(ctx):
    return owner_plane(ctx) * 8 + owner_slot(ctx)


def summing_level(plane):
    return 2 * (plane % 2) + (1 - plane // 2)


def split(value):
    high = value.astype(BF16)
    return high, (value - high.astype(F32)).astype(BF16)


def times_table(table, kind, k1, re, im):
    wide = jnp.concatenate([re, im], axis=1)
    high, low = split(wide)

    def paired(part):
        other = jnp.concatenate([part[:, LANES:], -part[:, :LANES]], axis=1)
        return jnp.concatenate([part, other], axis=0)

    high, low = paired(high), paired(low)
    t_high, t_low = table[kind, k1], table[kind + 1, k1]
    dot = functools.partial(jnp.dot, preferred_element_type=F32)
    return dot(t_high, high) + dot(t_low, high) + dot(t_high, low)


def body(
    q_hbm, k_hbm, v_hbm, g_hbm, filt_hbm, tab_hbm,
    qg_hbm, got_back, lag_hbm, total_ref,
    q_in, k_in, v_in, g_in, filt_part, tab,
    send_m, send_g, send_b, got_m, got_k, got_g, work, spec_k, spec_m, spec_g,
    got_conv, parts, summed, lag,
    tile_mine, tile_x, tile_row, tile_all,
    load_sem, out_sem, ksend, krecv, kxsend, kxrecv, msend, mrecv, gsend, grecv,
    csend, crecv, bsend, brecv, psend, precv, lsend, lrecv, xsend, xrecv, asend, arecv, own_sem,
):
    d = lax.axis_index("dp")
    c = lax.axis_index("ctx")
    plane = owner_plane(c)
    slot = owner_slot(c)
    mine = channel_block(c)
    z, y = c // 8, (c // 2) % 4

    loads = {}
    def load(name, index, source, target):
        loads[name] = pltpu.make_async_copy(source, target, load_sem.at[index])
        loads[name].start()

    load("filt", 0, filt_hbm.at[pl.ds(pl.multiple_of(d * 32, 32), 32)], filt_part)
    load("k", 1, k_hbm.at[0], k_in)
    load("v", 2, v_hbm.at[0], v_in)
    load("g", 3, g_hbm.at[0], g_in)
    load("q", 4, q_hbm.at[0], q_in)
    load("tab", 5, tab_hbm, tab)

    level = (z + y) % 4
    helper = 2 * (1 - level % 2) + level // 2

    def lag_source(h):
        hz = h // 2
        hy = 2 * (h % 2) + (d // 2 + hz) % 2
        return hz * 8 + hy * 2 + d % 2

    def lag_target(i, of_plane):
        tz = i // 2
        ty = (summing_level(of_plane) - tz + 4) % 4
        return tz * 8 + ty * 2 + i % 2

    barrier = pltpu.get_barrier_semaphore()

    def greet(i, carry):
        pl.semaphore_signal(barrier, inc=1, device_id=(d, (c + i) % CTX), device_id_type=MESH)
        return carry

    lax.fori_loop(1, CTX, greet, 0)
    for step in range(1, DP):
        pl.semaphore_signal(barrier, inc=1, device_id=((d + step) % DP, c), device_id_type=MESH)

    def greet_lag(h, carry):
        pl.semaphore_signal(barrier, inc=1, device_id=(helper, lag_source(h)), device_id_type=MESH)
        return carry

    lax.fori_loop(0, 8, greet_lag, 0)
    pl.semaphore_wait(barrier, 31 + 3 + 8)

    def each_peer(action, cores=(0, 2)):
        def of_core(step, carry):
            core = lax.rem(c + step, 2)
            for dz, dy in STEPS:
                action(lax.rem(z + dz, 4) * 8 + lax.rem(y + dy, 4) * 2 + core)
            return carry

        lax.fori_loop(*cores, of_core, 0)
        if cores[1] == 2:
            action(c + 1 - 2 * lax.rem(c, 2))

    def wait_bytes(ref, sem):
        pltpu.make_async_copy(ref, ref, sem).wait()

    quarter = pl.ds(pl.multiple_of(d * 32, 32), 32)

    def filt_cols(block):
        return filt_part.at[:, pl.ds(pl.multiple_of(block * LANES, LANES), LANES)]

    loads["filt"].wait()

    def send_filter(t):
        pltpu.make_async_remote_copy(
            src_ref=filt_cols(channel_block(t)), dst_ref=got_k.at[c, quarter],
            send_sem=ksend, recv_sem=krecv, device_id=(d, t), device_id_type=MESH,
        ).start()

    each_peer(send_filter)
    own_copy = pltpu.make_async_copy(filt_cols(mine), got_k.at[c, quarter], own_sem)
    own_copy.start()

    def product_out(left, right, store, target, ssem, rsem):
        def block(t):
            b = channel_block(t)
            cols = pl.ds(pl.multiple_of(b * LANES, LANES), LANES)
            store[b] = left[:, cols].astype(F32) * right[:, cols].astype(F32)
            pltpu.make_async_remote_copy(
                src_ref=store.at[b], dst_ref=target.at[c],
                send_sem=ssem, recv_sem=rsem, device_id=(d, t), device_id_type=MESH,
            ).start()

        each_peer(block)
        cols = pl.ds(pl.multiple_of(mine * LANES, LANES), LANES)
        target[c] = left[:, cols].astype(F32) * right[:, cols].astype(F32)

    loads["k"].wait()
    loads["v"].wait()
    product_out(k_in, v_in, send_m, got_m, msend, mrecv)

    own_copy.wait()
    wait_bytes(got_k.at[pl.ds(0, 31), quarter], krecv)
    share = []
    for step in range(1, DP):
        copy = pltpu.make_async_remote_copy(
            src_ref=got_k.at[:, quarter], dst_ref=got_k.at[:, quarter],
            send_sem=kxsend.at[step - 1], recv_sem=kxrecv.at[step - 1],
            device_id=((d + step) % DP, c), device_id_type=MESH,
        )
        copy.start()
        share.append(copy)

    loads["g"].wait()
    loads["q"].wait()
    product_out(g_in, q_in, send_g, got_g, gsend, grecv)

    def forward(got, spec, scale=None):
        def lead(i, carry):
            rows = pl.ds(pl.multiple_of(i * 8, 8), 8)
            x = [got[a, rows] for a in range(CTX)]
            if scale is not None:
                x = [value * scale for value in x]
            for k1, (re, im) in enumerate(lead_forward(x)):
                work[k1, rows, :LANES] = re
                work[k1, rows, LANES:] = im
            return carry

        lax.fori_loop(0, ROWS // 8, lead, 0)

        def rest(i, carry):
            for k1 in (2 * i, 2 * i + 1):
                spec[k1] = times_table(tab, 0, k1, work[k1, :, :LANES], work[k1, :, LANES:])
            return carry

        lax.fori_loop(0, CTX // 2, rest, 0)

    def inverse(left, right, conjugate, out):
        def rest(i, carry):
            for k1 in (2 * i, 2 * i + 1):
                lr, li = left[k1, :, :LANES], left[k1, :, LANES:]
                rr, ri = right[k1, :, :LANES], right[k1, :, LANES:]
                if conjugate:
                    re, im = lr * rr + li * ri, li * rr - lr * ri
                else:
                    re, im = lr * rr - li * ri, -(lr * ri + li * rr)
                work[k1] = times_table(tab, 2, k1, re, im)
            return carry

        lax.fori_loop(0, CTX // 2, rest, 0)

        def lead(i, carry):
            rows = pl.ds(pl.multiple_of(i * 8, 8), 8)
            v = [(work[k1, rows, :LANES], -work[k1, rows, LANES:]) for k1 in range(CTX)]
            for a, value in enumerate(lead_inverse(v)):
                out[a, rows] = value
            return carry

        lax.fori_loop(0, ROWS // 8, lead, 0)

    def send_back(source, target, ssem, rsem, cores=(0, 2)):
        def block(t):
            pltpu.make_async_remote_copy(
                src_ref=source.at[t], dst_ref=target.at[mine],
                send_sem=ssem, recv_sem=rsem, device_id=(d, t), device_id_type=MESH,
            ).start()

        each_peer(block, cores)
        if cores[1] != 2:
            return None
        copy = pltpu.make_async_copy(source.at[c], target.at[mine], own_sem)
        copy.start()
        return copy

    blocks = pl.ds(0, CTX - 1)
    loads["tab"].wait()
    wait_bytes(got_m.at[blocks], mrecv)
    forward(got_m, spec_m)
    for copy in share:
        copy.wait()
    forward(got_k, spec_k, PERIOD**-0.5)
    wait_bytes(send_m.at[blocks], msend)
    inverse(spec_k, spec_m, False, send_m)
    conv_own = send_back(send_m, got_conv, csend, crecv)

    wait_bytes(got_g.at[blocks], grecv)
    forward(got_g, spec_g)
    wait_bytes(send_g.at[blocks], gsend)
    inverse(spec_m, spec_g, True, send_g)

    share = []
    for step in range(1, DP):
        to = (d + step) % DP
        for pair in range(4):
            copy = pltpu.make_async_remote_copy(
                src_ref=send_g.at[pl.ds(lag_target(2 * pair, to), 2)],
                dst_ref=parts.at[step - 1, pl.ds(2 * pair, 2)],
                send_sem=psend.at[step - 1, pair], recv_sem=precv.at[step - 1, pair],
                device_id=(to, c), device_id_type=MESH,
            )
            copy.start()
            share.append(copy)

    inverse(spec_k, spec_g, True, send_b)
    conv_own.wait()
    send_back(send_b, got_back, bsend, brecv, (0, 1))

    wait_bytes(got_conv.at[blocks], crecv)

    def finish_conv(b, carry):
        cols = pl.ds(pl.multiple_of(b * LANES, LANES), LANES)
        q_in[:, cols] = (g_in[:, cols].astype(F32) * got_conv[b]).astype(BF16)
        return carry

    lax.fori_loop(0, CTX, finish_conv, 0)
    query_out = pltpu.make_async_copy(q_in, qg_hbm, out_sem.at[0])
    query_out.start()

    for copy in share:
        copy.wait()

    def add_up(i, carry):
        t = lag_target(i, d)
        summed[i] = (send_g[t] + parts[0, i]) + (parts[1, i] + parts[2, i])
        pltpu.make_async_remote_copy(
            src_ref=summed.at[i], dst_ref=lag.at[slot],
            send_sem=lsend, recv_sem=lrecv, device_id=(plane, t), device_id_type=MESH,
        ).start()
        return carry

    lax.fori_loop(0, 8, add_up, 0)
    back_own = send_back(send_b, got_back, bsend, brecv, (1, 2))
    wait_bytes(lag, lrecv)

    def measure(i, carry):
        squares, bad = carry
        value = lag[i].reshape(16, 8, LANES)
        finite = jnp.abs(value) < jnp.inf
        return (
            squares + jnp.sum(value * value, axis=0),
            bad + jnp.sum(jnp.where(finite, 0.0, 1.0), axis=0),
        )

    nothing = jnp.zeros((8, LANES), F32)
    squares, bad = lax.fori_loop(0, 8, measure, (nothing, nothing))
    tile_mine[:8] = squares
    tile_mine[8:] = bad
    share = []
    for step in range(1, DP):
        copy = pltpu.make_async_remote_copy(
            src_ref=tile_mine, dst_ref=tile_x.at[step - 1],
            send_sem=xsend.at[step - 1], recv_sem=xrecv.at[step - 1],
            device_id=((d + step) % DP, c), device_id_type=MESH,
        )
        copy.start()
        share.append(copy)
    for copy in share:
        copy.wait()
    tile_row[...] = (tile_mine[...] + tile_x[0]) + (tile_x[1] + tile_x[2])

    def spread(t):
        pltpu.make_async_remote_copy(
            src_ref=tile_row, dst_ref=tile_all.at[c],
            send_sem=asend, recv_sem=arecv, device_id=(d, t), device_id_type=MESH,
        ).start()

    each_peer(spread)
    tile_all[c] = tile_row[...]

    lag_out = pltpu.make_async_copy(lag, lag_hbm, out_sem.at[1])
    lag_out.start()
    wait_bytes(tile_all.at[blocks], arecv)
    total_ref[...] = jnp.sum(tile_all[...], axis=0)
    back_own.wait()
    wait_bytes(got_back.at[blocks], brecv)

    wait_bytes(got_k.at[blocks, quarter], ksend)
    wait_bytes(send_m.at[blocks], csend)
    wait_bytes(send_b.at[blocks], bsend)
    wait_bytes(summed, lsend)
    wait_bytes(tile_all.at[blocks], asend)
    query_out.wait()
    lag_out.wait()


def finish(
    qg_hbm, back_hbm, lag_hbm, total_ref, k_hbm, v_hbm, filt_hbm, m1_hbm, m2_hbm,
    query_hbm, key_hbm, value_hbm, nf_hbm, n1_hbm, n2_hbm,
    back, keys, values, query, lag, weight, first, second, in_sem, out_sem,
):
    d = lax.axis_index("dp")
    parts = keys.shape[0]
    width = keys.shape[2]
    per = back.shape[0] // parts

    def load(source, target, index):
        copy = pltpu.make_async_copy(source, target, in_sem.at[index])
        copy.start()
        return copy

    loads = []
    for part in range(parts):
        some, cols = pl.ds(part * per, per), pl.ds(part * width, width)
        loads.append((
            load(back_hbm.at[some], back.at[some], 3 * part),
            load(k_hbm.at[0, :, cols], keys.at[part], 3 * part + 1),
            load(v_hbm.at[0, :, cols], values.at[part], 3 * part + 2),
        ))
    state = [
        load(lag_hbm, lag, 3 * parts),
        load(filt_hbm.at[:, pl.ds(pl.multiple_of(d * 1024, 1024), 1024)], weight, 3 * parts + 1),
        load(m1_hbm, first, 3 * parts + 2),
        load(m2_hbm, second, 3 * parts + 3),
    ]
    query_in = load(qg_hbm, query, 3 * parts + 4)
    outs = []

    def store(source, target, index):
        copy = pltpu.make_async_copy(source, target, out_sem.at[index])
        copy.start()
        outs.append(copy)

    for part in range(parts):
        for copy in loads[part]:
            copy.wait()

        def gradients(i, carry):
            cols = pl.ds(pl.multiple_of(i * LANES, LANES), LANES)
            value = back[part * per + i]
            key_part = keys[part, :, cols].astype(F32)
            keys[part, :, cols] = (value * values[part, :, cols].astype(F32)).astype(BF16)
            values[part, :, cols] = (value * key_part).astype(BF16)
            return carry

        lax.fori_loop(0, per, gradients, 0)
        cols = pl.ds(part * width, width)
        store(keys.at[part], key_hbm.at[0, :, cols], 2 * part + 1)
        store(values.at[part], value_hbm.at[0, :, cols], 2 * part + 2)

    query_in.wait()
    store(query, query_hbm.at[0], 0)
    for copy in state:
        copy.wait()
    total_sq = jnp.sum(total_ref[:8])
    bad_count = jnp.sum(total_ref[8:])
    mean_sq = jnp.full((8, LANES), total_sq) * (1.0 / (PERIOD * 4096)) + 1e-06
    factor = jnp.minimum(1.0, 1.0 / jnp.sqrt(mean_sq))[:1]
    commit = (jnp.full((8, LANES), bad_count) == 0.0)[:1]

    def step(h, carry):
        cols = pl.ds(pl.multiple_of(h * LANES, LANES), LANES)
        clipped = lag[h] * factor
        m1, m2, filt = first[:, cols], second[:, cols], weight[:, cols]
        first_next = beta_first * m1 + (1.0 - beta_first) * clipped
        second_next = beta_second * m2 + (1.0 - beta_second) * clipped * clipped
        update = (
            first_next / correct_first / (jnp.sqrt(second_next / correct_second) + adam_epsilon)
            + decay_rate * filt
        )
        weight[:, cols] = jnp.where(commit, filt - learn_rate * update, filt)
        first[:, cols] = jnp.where(commit, first_next, m1)
        second[:, cols] = jnp.where(commit, second_next, m2)
        return carry

    lax.fori_loop(0, 8, step, 0)
    store(weight, nf_hbm, 2 * parts + 1)
    store(first, n1_hbm, 2 * parts + 2)
    store(second, n2_hbm, 2 * parts + 3)
    for copy in outs:
        copy.wait()


def on_device(query_act, key_act, value_act, out_grad, filter_weight, first_moment, second_moment):
    table = jnp.asarray(dft_tables())
    block = (CTX, ROWS, LANES)
    wide = (CTX, ROWS, 2 * LANES)
    vmem = pltpu.VMEM
    dma = pltpu.SemaphoreType.DMA
    anywhere = pl.BlockSpec(memory_space=pltpu.HBM)
    either = pl.BlockSpec(memory_space=pl.ANY)
    stream = jax.ShapeDtypeStruct(query_act.shape, BF16)
    state = jax.ShapeDtypeStruct(first_moment.shape, F32)
    query_grad, back_in, lag_grad, total = pl.pallas_call(
        body,
        out_shape=(
            jax.ShapeDtypeStruct((ROWS, 4096), BF16),
            jax.ShapeDtypeStruct(block, F32),
            jax.ShapeDtypeStruct((8, ROWS, LANES), F32),
            jax.ShapeDtypeStruct((16, LANES), F32),
        ),
        in_specs=[anywhere] * 6,
        out_specs=(either, either, either, pl.BlockSpec(memory_space=pltpu.VMEM)),
        scratch_shapes=[
            vmem((ROWS, 4096), BF16), vmem((ROWS, 4096), BF16),
            vmem((ROWS, 4096), BF16), vmem((ROWS, 4096), BF16),
            vmem((32, 4096), F32),
            vmem((4,) + wide, BF16),
            vmem(block, F32), vmem(block, F32), vmem(block, F32),
            vmem(block, F32), vmem(block, F32), vmem(block, F32),
            vmem(wide, F32), vmem(wide, F32), vmem(wide, F32), vmem(wide, F32),
            vmem(block, F32),
            vmem((3, 8, ROWS, LANES), F32), vmem((8, ROWS, LANES), F32), vmem((8, ROWS, LANES), F32),
            vmem((16, LANES), F32), vmem((3, 16, LANES), F32), vmem((16, LANES), F32),
            vmem((CTX, 16, LANES), F32),
            dma((6,)), dma((2,)), dma, dma, dma((3,)), dma((3,)), dma, dma, dma, dma,
            dma, dma, dma, dma, dma((3, 4)), dma((3, 4)), dma, dma, dma((3,)), dma((3,)), dma, dma, dma,
        ],
        compiler_params=pltpu.CompilerParams(
            collective_id=0, has_side_effects=True, vmem_limit_bytes=VMEM_MIB * 2**20
        ),
    )(query_act, key_act, value_act, out_grad, filter_weight, table)
    cuts = 4
    return pl.pallas_call(
        finish,
        out_shape=(stream, stream, stream, state, state, state),
        in_specs=[either] * 3 + [pl.BlockSpec(memory_space=pltpu.VMEM)] + [anywhere] * 5,
        out_specs=(anywhere,) * 6,
        scratch_shapes=[
            vmem(block, F32), vmem((cuts, ROWS, 4096 // cuts), BF16), vmem((cuts, ROWS, 4096 // cuts), BF16),
            vmem((ROWS, 4096), BF16),
            vmem((8, ROWS, LANES), F32), vmem((ROWS, 1024), F32), vmem((ROWS, 1024), F32), vmem((ROWS, 1024), F32),
            dma((3 * cuts + 5,)), dma((2 * cuts + 4,)),
        ],
        compiler_params=pltpu.CompilerParams(vmem_limit_bytes=VMEM_MIB * 2**20),
    )(query_grad, back_in, lag_grad, total, key_act, value_act, filter_weight, first_moment, second_moment)


def solution(mesh):
    return jax.shard_map(
        on_device,
        mesh=mesh,
        in_specs=(
            P("dp", "ctx", None),
            P("dp", "ctx", None),
            P("dp", "ctx", None),
            P("dp", "ctx", None),
            P("ctx", None),
            P("ctx", "dp"),
            P("ctx", "dp"),
        ),
        out_specs=(
            P("dp", "ctx", None),
            P("dp", "ctx", None),
            P("dp", "ctx", None),
            P("ctx", "dp"),
            P("ctx", "dp"),
            P("ctx", "dp"),
        ),
        check_vma=False,
    )
```

```python
import functools
import math

import jax
import jax.numpy as jnp
import numpy as np
from jax import lax
from jax.experimental import pallas as pl
from jax.experimental.pallas import tpu as pltpu
from jax.sharding import PartitionSpec as P

MESH = pl.DeviceIdType.MESH
F32 = jnp.float32
BF16 = jnp.bfloat16

DP = 4
CTX = 32
ROWS = 128
LANES = 128
VMEM_MIB = 51
BACK_EARLY = 7
PERIOD = CTX * ROWS
STEPS = (
    (2, 2), (2, 3), (3, 2), (2, 1), (1, 2), (2, 0), (0, 2), (1, 1),
    (3, 3), (1, 3), (3, 1), (0, 1), (1, 0), (0, 3), (3, 0),
)

beta_first = 0.9
beta_second = 0.95
learn_rate = 0.01
decay_rate = 0.1
adam_epsilon = 1e-08
correct_first = 0.9999734386011124
correct_second = 0.994079470779666


def dft_tables():
    k1 = np.arange(CTX)[:, None, None]
    m = np.arange(ROWS)[None, :, None]
    j = np.arange(ROWS)[None, None, :]
    turns = (j * (4 * k1 + 1 + 4 * CTX * m)) % (4 * PERIOD)
    angle = turns * (2.0 * np.pi / (4 * PERIOD))
    cosine, sine = np.cos(angle), np.sin(angle)
    forward = np.concatenate([cosine, sine], axis=2)
    inverse = np.concatenate([cosine.swapaxes(1, 2), sine.swapaxes(1, 2)], axis=2) / PERIOD
    out = []
    for table in (forward, inverse):
        high = table.astype(jnp.bfloat16)
        low = (table - high.astype(np.float64)).astype(jnp.bfloat16)
        out += [high, low]
    return np.stack(out)


def rotated(value, turn):
    re, im = value
    turn = turn % 1.0
    if turn == 0.0:
        return value
    c, s = math.cos(2 * math.pi * turn), math.sin(2 * math.pi * turn)
    return (re * c + im * s, im * c - re * s)


def dft8(v, sign):
    half = math.sqrt(0.5)

    def add(a, b):
        return (a[0] + b[0], a[1] + b[1])

    def sub(a, b):
        return (a[0] - b[0], a[1] - b[1])

    def quarter(a):
        return (a[1], -a[0]) if sign > 0 else (-a[1], a[0])

    def sub_quarter(a, b):
        if sign > 0:
            return (a[0] + b[1], a[1] - b[0]), (a[0] - b[1], a[1] + b[0])
        return (a[0] - b[1], a[1] + b[0]), (a[0] + b[1], a[1] - b[0])

    def dft4(a, b, c, d):
        s0, s1 = add(a, c), sub(a, c)
        s2, s3 = add(b, d), sub(b, d)
        y1, y3 = sub_quarter(s1, s3)
        return add(s0, s2), y1, sub(s0, s2), y3

    e = dft4(v[0], v[2], v[4], v[6])
    o = dft4(v[1], v[3], v[5], v[7])
    if sign > 0:
        o1 = ((o[1][0] + o[1][1]) * half, (o[1][1] - o[1][0]) * half)
        o3 = ((o[3][1] - o[3][0]) * half, (o[3][0] + o[3][1]) * (-half))
    else:
        o1 = ((o[1][0] - o[1][1]) * half, (o[1][1] + o[1][0]) * half)
        o3 = ((o[3][0] + o[3][1]) * (-half), (o[3][0] - o[3][1]) * half)
    y2, y6 = sub_quarter(e[2], o[2])
    return [
        add(e[0], o[0]), add(e[1], o1), y2, add(e[3], o3),
        sub(e[0], o[0]), sub(e[1], o1), y6, sub(e[3], o3),
    ]


def lead_forward(x):
    c1, s1 = math.cos(math.pi / 8), math.sin(math.pi / 8)
    half = math.sqrt(0.5)
    u = [[None] * 8 for _ in range(4)]
    for a0 in range(8):
        x0, x1, x2, x3 = x[a0], x[a0 + 8], x[a0 + 16], x[a0 + 24]
        p1r, p1i = x1 * c1, x1 * s1
        p3r, p3i = x3 * s1, x3 * c1
        s = x2 * half
        ep, em = x0 + s, x0 - s
        sr, si = p1r + p3r, p1i + p3i
        dr, di = p1r - p3r, p1i - p3i
        u[0][a0] = (ep + sr, -(s + si))
        u[2][a0] = (ep - sr, si - s)
        u[1][a0] = (em - di, s - dr)
        u[3][a0] = (em + di, s + dr)
    out = [None] * 32
    for q in range(4):
        y = dft8([rotated(u[q][a0], a0 * (4 * q + 1) / 128.0) for a0 in range(8)], 1)
        for r in range(8):
            out[q + 4 * r] = y[r]
    return out


def lead_inverse(v):
    c1, s1 = math.cos(math.pi / 8), math.sin(math.pi / 8)
    half = math.sqrt(0.5)
    u = []
    for q in range(4):
        t = dft8([v[q + 4 * r] for r in range(8)], -1)
        u.append([rotated(t[a0], -a0 * (4 * q + 1) / 128.0) for a0 in range(8)])
    out = [None] * 32
    for a0 in range(8):
        (r0, i0), (r1, i1), (r2, i2), (r3, i3) = u[0][a0], u[1][a0], u[2][a0], u[3][a0]
        ar, ai, br, bi = r0 + r2, i0 + i2, r0 - r2, i0 - i2
        cr, ci, dr, di = r1 + r3, i1 + i3, r1 - r3, i1 - i3
        out[a0] = ar + cr
        out[a0 + 8] = (br - di) * c1 - (bi + dr) * s1
        out[a0 + 16] = ((ar - cr) - (ai - ci)) * half
        out[a0 + 24] = (br + di) * s1 - (bi - dr) * c1
    return out


def owner_plane(ctx):
    z, y, core = ctx // 8, (ctx // 2) % 4, ctx % 2
    return 2 * ((z + y) % 2) + core


def owner_slot(ctx):
    z, y = ctx // 8, (ctx // 2) % 4
    return 2 * z + y // 2


def channel_block(ctx):
    return owner_plane(ctx) * 8 + owner_slot(ctx)


def summing_level(plane):
    return 2 * (plane % 2) + (1 - plane // 2)


def split(value):
    high = value.astype(BF16)
    return high, (value - high.astype(F32)).astype(BF16)


def times_table(table, kind, k1, re, im):
    wide = jnp.concatenate([re, im], axis=1)
    high, low = split(wide)

    def paired(part):
        other = jnp.concatenate([part[:, LANES:], -part[:, :LANES]], axis=1)
        return jnp.concatenate([part, other], axis=0)

    high, low = paired(high), paired(low)
    t_high, t_low = table[kind, k1], table[kind + 1, k1]
    dot = functools.partial(jnp.dot, preferred_element_type=F32)
    return dot(t_high, high) + dot(t_low, high) + dot(t_high, low)


def body(
    q_hbm, k_hbm, v_hbm, g_hbm, filt_hbm, tab_hbm,
    qg_hbm, got_back, lag_hbm, own_hbm, total_ref,
    q_in, k_in, v_in, g_in, filt_part, tab,
    send_m, send_g, send_b, got_m, got_k, got_g, work, spec_k, spec_m, spec_g,
    got_conv, parts, summed, lag,
    tile_mine, tile_x, tile_row, tile_all,
    load_sem, out_sem, ksend, krecv, kxsend, kxrecv, msend, mrecv, gsend, grecv,
    csend, crecv, bsend, brecv, psend, precv, lsend, lrecv, xsend, xrecv, asend, arecv, own_sem,
):
    d = lax.axis_index("dp")
    c = lax.axis_index("ctx")
    plane = owner_plane(c)
    slot = owner_slot(c)
    mine = channel_block(c)
    z, y = c // 8, (c // 2) % 4

    loads = {}
    def load(name, index, source, target):
        loads[name] = pltpu.make_async_copy(source, target, load_sem.at[index])
        loads[name].start()

    load("filt", 0, filt_hbm.at[pl.ds(pl.multiple_of(d * 32, 32), 32)], filt_part)
    load("k", 1, k_hbm.at[0], k_in)
    load("v", 2, v_hbm.at[0], v_in)
    load("g", 3, g_hbm.at[0], g_in)
    load("q", 4, q_hbm.at[0], q_in)
    load("tab", 5, tab_hbm, tab)
    load("own", 6, filt_hbm.at[:, pl.ds(pl.multiple_of(d * 1024, 1024), 1024)], own_hbm)

    level = (z + y) % 4
    helper = 2 * (1 - level % 2) + level // 2

    def lag_source(h):
        hz = h // 2
        hy = 2 * (h % 2) + (d // 2 + hz) % 2
        return hz * 8 + hy * 2 + d % 2

    def lag_target(i, of_plane):
        tz = i // 2
        ty = (summing_level(of_plane) - tz + 4) % 4
        return tz * 8 + ty * 2 + i % 2

    barrier = pltpu.get_barrier_semaphore()

    def greet(i, carry):
        pl.semaphore_signal(barrier, inc=1, device_id=(d, (c + i) % CTX), device_id_type=MESH)
        return carry

    lax.fori_loop(1, CTX, greet, 0)
    for step in range(1, DP):
        pl.semaphore_signal(barrier, inc=1, device_id=((d + step) % DP, c), device_id_type=MESH)

    def greet_lag(h, carry):
        pl.semaphore_signal(barrier, inc=1, device_id=(helper, lag_source(h)), device_id_type=MESH)
        return carry

    lax.fori_loop(0, 8, greet_lag, 0)
    pl.semaphore_wait(barrier, 31 + 3 + 8)

    def some_peers(action, step, first, last):
        core = lax.rem(c + step, 2)
        for dz, dy in STEPS[first:last]:
            action(lax.rem(z + dz, 4) * 8 + lax.rem(y + dy, 4) * 2 + core)

    def sibling(action):
        action(c + 1 - 2 * lax.rem(c, 2))

    def each_peer(action):
        def of_core(step, carry):
            some_peers(action, step, 0, len(STEPS))
            return carry

        lax.fori_loop(0, 2, of_core, 0)
        sibling(action)

    def wait_bytes(ref, sem):
        pltpu.make_async_copy(ref, ref, sem).wait()

    quarter = pl.ds(pl.multiple_of(d * 32, 32), 32)

    def filt_cols(block):
        return filt_part.at[:, pl.ds(pl.multiple_of(block * LANES, LANES), LANES)]

    loads["filt"].wait()

    def send_filter(t):
        pltpu.make_async_remote_copy(
            src_ref=filt_cols(channel_block(t)), dst_ref=got_k.at[c, quarter],
            send_sem=ksend, recv_sem=krecv, device_id=(d, t), device_id_type=MESH,
        ).start()

    each_peer(send_filter)
    own_copy = pltpu.make_async_copy(filt_cols(mine), got_k.at[c, quarter], own_sem)
    own_copy.start()

    def product(left, right, b):
        cols = pl.ds(pl.multiple_of(b * LANES, LANES), LANES)
        return left[:, cols].astype(F32) * right[:, cols].astype(F32)

    def send_block(t, store, target, ssem, rsem):
        pltpu.make_async_remote_copy(
            src_ref=store.at[channel_block(t)], dst_ref=target.at[c],
            send_sem=ssem, recv_sem=rsem, device_id=(d, t), device_id_type=MESH,
        ).start()

    loads["k"].wait()
    loads["v"].wait()

    def mixed(b, carry):
        send_m[b] = product(k_in, v_in, b)
        return carry

    lax.fori_loop(0, CTX, mixed, 0)
    got_m[c] = send_m[mine]

    blocks = pl.ds(0, CTX - 1)
    each_peer(lambda t: send_block(t, send_m, got_m, msend, mrecv))

    loads["g"].wait()
    loads["q"].wait()

    def gated(b, carry):
        send_g[b] = product(g_in, q_in, b)
        return carry

    lax.fori_loop(0, CTX, gated, 0)
    got_g[c] = send_g[mine]

    own_copy.wait()
    wait_bytes(got_k.at[pl.ds(0, 31), quarter], krecv)
    share = []
    for step in range(1, DP):
        copy = pltpu.make_async_remote_copy(
            src_ref=got_k.at[:, quarter], dst_ref=got_k.at[:, quarter],
            send_sem=kxsend.at[step - 1], recv_sem=kxrecv.at[step - 1],
            device_id=((d + step) % DP, c), device_id_type=MESH,
        )
        copy.start()
        share.append(copy)

    wait_bytes(send_m.at[blocks], msend)
    each_peer(lambda t: send_block(t, send_g, got_g, gsend, grecv))

    def forward(got, spec, scale=None):
        def lead(i, carry):
            rows = pl.ds(pl.multiple_of(i * 8, 8), 8)
            x = [got[a, rows] for a in range(CTX)]
            if scale is not None:
                x = [value * scale for value in x]
            for k1, (re, im) in enumerate(lead_forward(x)):
                work[k1, rows, :LANES] = re
                work[k1, rows, LANES:] = im
            return carry

        lax.fori_loop(0, ROWS // 8, lead, 0)

        def rest(i, carry):
            for k1 in (2 * i, 2 * i + 1):
                spec[k1] = times_table(tab, 0, k1, work[k1, :, :LANES], work[k1, :, LANES:])
            return carry

        lax.fori_loop(0, CTX // 2, rest, 0)

    def inverse(left, right, conjugate, out):
        def rest(i, carry):
            for k1 in (2 * i, 2 * i + 1):
                lr, li = left[k1, :, :LANES], left[k1, :, LANES:]
                rr, ri = right[k1, :, :LANES], right[k1, :, LANES:]
                if conjugate:
                    re, im = lr * rr + li * ri, li * rr - lr * ri
                else:
                    re, im = lr * rr - li * ri, -(lr * ri + li * rr)
                work[k1] = times_table(tab, 2, k1, re, im)
            return carry

        lax.fori_loop(0, CTX // 2, rest, 0)

        def lead(i, carry):
            rows = pl.ds(pl.multiple_of(i * 8, 8), 8)
            v = [(work[k1, rows, :LANES], -work[k1, rows, LANES:]) for k1 in range(CTX)]
            for a, value in enumerate(lead_inverse(v)):
                out[a, rows] = value
            return carry

        lax.fori_loop(0, ROWS // 8, lead, 0)

    def result_block(source, target, ssem, rsem):
        def send(t):
            pltpu.make_async_remote_copy(
                src_ref=source.at[t], dst_ref=target.at[mine],
                send_sem=ssem, recv_sem=rsem, device_id=(d, t), device_id_type=MESH,
            ).start()

        return send

    def keep_own(source, target):
        copy = pltpu.make_async_copy(source.at[c], target.at[mine], own_sem)
        copy.start()
        return copy

    loads["tab"].wait()
    wait_bytes(got_m.at[blocks], mrecv)
    forward(got_m, spec_m)
    for copy in share:
        copy.wait()
    forward(got_k, spec_k, PERIOD**-0.5)
    inverse(spec_k, spec_m, False, send_m)
    wait_bytes(send_g.at[blocks], gsend)
    each_peer(result_block(send_m, got_conv, csend, crecv))
    conv_own = keep_own(send_m, got_conv)

    wait_bytes(got_g.at[blocks], grecv)
    forward(got_g, spec_g)
    inverse(spec_m, spec_g, True, send_g)

    share = []
    for step in range(1, DP):
        to = (d + step) % DP
        for pair in range(4):
            copy = pltpu.make_async_remote_copy(
                src_ref=send_g.at[pl.ds(lag_target(2 * pair, to), 2)],
                dst_ref=parts.at[step - 1, pl.ds(2 * pair, 2)],
                send_sem=psend.at[step - 1, pair], recv_sem=precv.at[step - 1, pair],
                device_id=(to, c), device_id_type=MESH,
            )
            copy.start()
            share.append(copy)

    inverse(spec_k, spec_g, True, send_b)
    conv_own.wait()
    wait_bytes(send_m.at[blocks], csend)
    back_block = result_block(send_b, got_back, bsend, brecv)
    some_peers(back_block, 0, 0, 15)

    wait_bytes(got_conv.at[blocks], crecv)

    def finish_conv(b, carry):
        cols = pl.ds(pl.multiple_of(b * LANES, LANES), LANES)
        q_in[:, cols] = (g_in[:, cols].astype(F32) * got_conv[b]).astype(BF16)
        return carry

    lax.fori_loop(0, CTX, finish_conv, 0)
    query_out = pltpu.make_async_copy(q_in, qg_hbm, out_sem.at[0])
    query_out.start()

    for copy in share:
        copy.wait()

    def add_up(i, carry):
        squares, bad = carry
        value = (send_g[lag_target(i, d)] + parts[0, i]) + (parts[1, i] + parts[2, i])
        summed[i] = value
        value = value.reshape(16, 8, LANES)
        finite = jnp.abs(value) < jnp.inf
        return (
            squares + jnp.sum(value * value, axis=0),
            bad + jnp.sum(jnp.where(finite, 0.0, 1.0), axis=0),
        )

    nothing = jnp.zeros((8, LANES), F32)
    squares, bad = lax.fori_loop(0, 8, add_up, (nothing, nothing))
    tile_mine[:8] = squares
    tile_mine[8:] = bad
    share = []
    for step in range(1, DP):
        copy = pltpu.make_async_remote_copy(
            src_ref=tile_mine, dst_ref=tile_x.at[step - 1],
            send_sem=xsend.at[step - 1], recv_sem=xrecv.at[step - 1],
            device_id=((d + step) % DP, c), device_id_type=MESH,
        )
        copy.start()
        share.append(copy)

    def send_lag(i, carry):
        pltpu.make_async_remote_copy(
            src_ref=summed.at[i], dst_ref=lag.at[slot],
            send_sem=lsend, recv_sem=lrecv, device_id=(plane, lag_target(i, d)), device_id_type=MESH,
        ).start()
        return carry

    lax.fori_loop(0, 8, send_lag, 0)
    some_peers(back_block, 1, 0, BACK_EARLY)
    for copy in share:
        copy.wait()
    tile_row[...] = (tile_mine[...] + tile_x[0]) + (tile_x[1] + tile_x[2])

    def spread(t):
        pltpu.make_async_remote_copy(
            src_ref=tile_row, dst_ref=tile_all.at[c],
            send_sem=asend, recv_sem=arecv, device_id=(d, t), device_id_type=MESH,
        ).start()

    each_peer(spread)
    tile_all[c] = tile_row[...]
    some_peers(back_block, 1, BACK_EARLY, 15)
    sibling(back_block)
    back_own = keep_own(send_b, got_back)
    wait_bytes(lag, lrecv)

    lag_out = pltpu.make_async_copy(lag, lag_hbm, out_sem.at[1])
    lag_out.start()
    wait_bytes(tile_all.at[blocks], arecv)
    total_ref[...] = jnp.sum(tile_all[...], axis=0)
    back_own.wait()
    wait_bytes(got_back.at[blocks], brecv)

    wait_bytes(got_k.at[blocks, quarter], ksend)
    wait_bytes(send_b.at[blocks], bsend)
    wait_bytes(summed, lsend)
    wait_bytes(tile_all.at[blocks], asend)
    query_out.wait()
    lag_out.wait()
    loads["own"].wait()


def finish(
    query_ref, back_ref, lag_ref, total_ref, k_ref, v_ref, filt_ref, m1_ref, m2_ref,
    query_hbm, key_hbm, value_hbm, nf_hbm, n1_hbm, n2_hbm,
    keys, values, weight, first, second, out_sem,
):
    parts = keys.shape[0]
    width = keys.shape[2]
    per = width // LANES
    outs = []

    def store(source, target, index):
        copy = pltpu.make_async_copy(source, target, out_sem.at[index])
        copy.start()
        outs.append(copy)

    store(query_ref, query_hbm.at[0], 0)
    for part in range(parts):

        def gradients(i, carry):
            cols = pl.ds(pl.multiple_of(i * LANES, LANES), LANES)
            wide_cols = pl.ds(pl.multiple_of(part * width + i * LANES, LANES), LANES)
            value = back_ref[part * per + i]
            keys[part, :, cols] = (value * v_ref[0, :, wide_cols].astype(F32)).astype(BF16)
            values[part, :, cols] = (value * k_ref[0, :, wide_cols].astype(F32)).astype(BF16)
            return carry

        lax.fori_loop(0, per, gradients, 0)
        cols = pl.ds(part * width, width)
        store(keys.at[part], key_hbm.at[0, :, cols], 2 * part + 1)
        store(values.at[part], value_hbm.at[0, :, cols], 2 * part + 2)

    total_sq = jnp.sum(total_ref[:8])
    bad_count = jnp.sum(total_ref[8:])
    mean_sq = jnp.full((8, LANES), total_sq) * (1.0 / (PERIOD * 4096)) + 1e-06
    factor = jnp.minimum(1.0, 1.0 / jnp.sqrt(mean_sq))[:1]
    commit = (jnp.full((8, LANES), bad_count) == 0.0)[:1]

    def step(h, carry):
        cols = pl.ds(pl.multiple_of(h * LANES, LANES), LANES)
        clipped = lag_ref[h] * factor
        m1, m2, filt = m1_ref[:, cols], m2_ref[:, cols], filt_ref[:, cols]
        first_next = beta_first * m1 + (1.0 - beta_first) * clipped
        second_next = beta_second * m2 + (1.0 - beta_second) * clipped * clipped
        update = (
            first_next / correct_first / (jnp.sqrt(second_next / correct_second) + adam_epsilon)
            + decay_rate * filt
        )
        weight[:, cols] = jnp.where(commit, filt - learn_rate * update, filt)
        first[:, cols] = jnp.where(commit, first_next, m1)
        second[:, cols] = jnp.where(commit, second_next, m2)
        return carry

    lax.fori_loop(0, 8, step, 0)
    store(weight, nf_hbm, 2 * parts + 1)
    store(first, n1_hbm, 2 * parts + 2)
    store(second, n2_hbm, 2 * parts + 3)
    for copy in outs:
        copy.wait()


def on_device(query_act, key_act, value_act, out_grad, filter_weight, first_moment, second_moment):
    table = jnp.asarray(dft_tables())
    block = (CTX, ROWS, LANES)
    wide = (CTX, ROWS, 2 * LANES)
    vmem = pltpu.VMEM
    dma = pltpu.SemaphoreType.DMA
    anywhere = pl.BlockSpec(memory_space=pltpu.HBM)
    either = pl.BlockSpec(memory_space=pl.ANY)
    stream = jax.ShapeDtypeStruct(query_act.shape, BF16)
    state = jax.ShapeDtypeStruct(first_moment.shape, F32)
    query_grad, back_in, lag_grad, own_filter, total = pl.pallas_call(
        body,
        out_shape=(
            jax.ShapeDtypeStruct((ROWS, 4096), BF16),
            jax.ShapeDtypeStruct(block, F32),
            jax.ShapeDtypeStruct((8, ROWS, LANES), F32),
            state,
            jax.ShapeDtypeStruct((16, LANES), F32),
        ),
        in_specs=[anywhere] * 6,
        out_specs=(either, either, either, either, pl.BlockSpec(memory_space=pltpu.VMEM)),
        scratch_shapes=[
            vmem((ROWS, 4096), BF16), vmem((ROWS, 4096), BF16),
            vmem((ROWS, 4096), BF16), vmem((ROWS, 4096), BF16),
            vmem((32, 4096), F32),
            vmem((4,) + wide, BF16),
            vmem(block, F32), vmem(block, F32), vmem(block, F32),
            vmem(block, F32), vmem(block, F32), vmem(block, F32),
            vmem(wide, F32), vmem(wide, F32), vmem(wide, F32), vmem(wide, F32),
            vmem(block, F32),
            vmem((3, 8, ROWS, LANES), F32), vmem((8, ROWS, LANES), F32), vmem((8, ROWS, LANES), F32),
            vmem((16, LANES), F32), vmem((3, 16, LANES), F32), vmem((16, LANES), F32),
            vmem((CTX, 16, LANES), F32),
            dma((7,)), dma((2,)), dma, dma, dma((3,)), dma((3,)), dma, dma, dma, dma,
            dma, dma, dma, dma, dma((3, 4)), dma((3, 4)), dma, dma, dma((3,)), dma((3,)), dma, dma, dma,
        ],
        compiler_params=pltpu.CompilerParams(
            collective_id=0, has_side_effects=True, vmem_limit_bytes=VMEM_MIB * 2**20
        ),
    )(query_act, key_act, value_act, out_grad, filter_weight, table)
    cuts = 4
    local = pl.BlockSpec(memory_space=pltpu.VMEM)
    return pl.pallas_call(
        finish,
        out_shape=(stream, stream, stream, state, state, state),
        in_specs=[local] * 9,
        out_specs=(anywhere,) * 6,
        scratch_shapes=[
            vmem((cuts, ROWS, 4096 // cuts), BF16), vmem((cuts, ROWS, 4096 // cuts), BF16),
            vmem((ROWS, 1024), F32), vmem((ROWS, 1024), F32), vmem((ROWS, 1024), F32),
            dma((2 * cuts + 4,)),
        ],
        compiler_params=pltpu.CompilerParams(vmem_limit_bytes=16 * 2**20),
    )(query_grad, back_in, lag_grad, total, key_act, value_act, own_filter, first_moment, second_moment)


def solution(mesh):
    return jax.shard_map(
        on_device,
        mesh=mesh,
        in_specs=(
            P("dp", "ctx", None),
            P("dp", "ctx", None),
            P("dp", "ctx", None),
            P("dp", "ctx", None),
            P("ctx", None),
            P("ctx", "dp"),
            P("ctx", "dp"),
        ),
        out_specs=(
            P("dp", "ctx", None),
            P("dp", "ctx", None),
            P("dp", "ctx", None),
            P("ctx", "dp"),
            P("ctx", "dp"),
            P("ctx", "dp"),
        ),
        check_vma=False,
    )
```

```python
import functools
import math

import jax
import jax.numpy as jnp
import numpy as np
from jax import lax
from jax.experimental import pallas as pl
from jax.experimental.pallas import tpu as pltpu
from jax.sharding import PartitionSpec as P

MESH = pl.DeviceIdType.MESH
F32 = jnp.float32
BF16 = jnp.bfloat16

DP = 4
CTX = 32
ROWS = 128
LANES = 128
VMEM_MIB = 51
BACK_EARLY = 7
PERIOD = CTX * ROWS
STEPS = (
    (2, 2), (2, 3), (3, 2), (2, 1), (1, 2), (2, 0), (0, 2), (1, 1),
    (3, 3), (1, 3), (3, 1), (0, 1), (1, 0), (0, 3), (3, 0),
)

beta_first = 0.9
beta_second = 0.95
learn_rate = 0.01
decay_rate = 0.1
adam_epsilon = 1e-08
correct_first = 0.9999734386011124
correct_second = 0.994079470779666


def dft_tables():
    k1 = np.arange(CTX)[:, None, None]
    m = np.arange(ROWS)[None, :, None]
    j = np.arange(ROWS)[None, None, :]
    turns = (j * (4 * k1 + 1 + 4 * CTX * m)) % (4 * PERIOD)
    angle = turns * (2.0 * np.pi / (4 * PERIOD))
    cosine, sine = np.cos(angle), np.sin(angle)
    forward = np.concatenate([cosine, sine], axis=2)
    inverse = np.concatenate([cosine.swapaxes(1, 2), sine.swapaxes(1, 2)], axis=2) / PERIOD
    out = []
    for table in (forward, inverse):
        high = table.astype(jnp.bfloat16)
        low = (table - high.astype(np.float64)).astype(jnp.bfloat16)
        out += [high, low]
    return np.stack(out)


def rotated(value, turn):
    re, im = value
    turn = turn % 1.0
    if turn == 0.0:
        return value
    c, s = math.cos(2 * math.pi * turn), math.sin(2 * math.pi * turn)
    return (re * c + im * s, im * c - re * s)


def dft8(v, sign):
    half = math.sqrt(0.5)

    def add(a, b):
        return (a[0] + b[0], a[1] + b[1])

    def sub(a, b):
        return (a[0] - b[0], a[1] - b[1])

    def quarter(a):
        return (a[1], -a[0]) if sign > 0 else (-a[1], a[0])

    def sub_quarter(a, b):
        if sign > 0:
            return (a[0] + b[1], a[1] - b[0]), (a[0] - b[1], a[1] + b[0])
        return (a[0] - b[1], a[1] + b[0]), (a[0] + b[1], a[1] - b[0])

    def dft4(a, b, c, d):
        s0, s1 = add(a, c), sub(a, c)
        s2, s3 = add(b, d), sub(b, d)
        y1, y3 = sub_quarter(s1, s3)
        return add(s0, s2), y1, sub(s0, s2), y3

    e = dft4(v[0], v[2], v[4], v[6])
    o = dft4(v[1], v[3], v[5], v[7])
    if sign > 0:
        o1 = ((o[1][0] + o[1][1]) * half, (o[1][1] - o[1][0]) * half)
        o3 = ((o[3][1] - o[3][0]) * half, (o[3][0] + o[3][1]) * (-half))
    else:
        o1 = ((o[1][0] - o[1][1]) * half, (o[1][1] + o[1][0]) * half)
        o3 = ((o[3][0] + o[3][1]) * (-half), (o[3][0] - o[3][1]) * half)
    y2, y6 = sub_quarter(e[2], o[2])
    return [
        add(e[0], o[0]), add(e[1], o1), y2, add(e[3], o3),
        sub(e[0], o[0]), sub(e[1], o1), y6, sub(e[3], o3),
    ]


def lead_forward(x):
    c1, s1 = math.cos(math.pi / 8), math.sin(math.pi / 8)
    half = math.sqrt(0.5)
    u = [[None] * 8 for _ in range(4)]
    for a0 in range(8):
        x0, x1, x2, x3 = x[a0], x[a0 + 8], x[a0 + 16], x[a0 + 24]
        p1r, p1i = x1 * c1, x1 * s1
        p3r, p3i = x3 * s1, x3 * c1
        s = x2 * half
        ep, em = x0 + s, x0 - s
        sr, si = p1r + p3r, p1i + p3i
        dr, di = p1r - p3r, p1i - p3i
        u[0][a0] = (ep + sr, -(s + si))
        u[2][a0] = (ep - sr, si - s)
        u[1][a0] = (em - di, s - dr)
        u[3][a0] = (em + di, s + dr)
    out = [None] * 32
    for q in range(4):
        y = dft8([rotated(u[q][a0], a0 * (4 * q + 1) / 128.0) for a0 in range(8)], 1)
        for r in range(8):
            out[q + 4 * r] = y[r]
    return out


def lead_inverse(v):
    c1, s1 = math.cos(math.pi / 8), math.sin(math.pi / 8)
    half = math.sqrt(0.5)
    u = []
    for q in range(4):
        t = dft8([v[q + 4 * r] for r in range(8)], -1)
        u.append([rotated(t[a0], -a0 * (4 * q + 1) / 128.0) for a0 in range(8)])
    out = [None] * 32
    for a0 in range(8):
        (r0, i0), (r1, i1), (r2, i2), (r3, i3) = u[0][a0], u[1][a0], u[2][a0], u[3][a0]
        ar, ai, br, bi = r0 + r2, i0 + i2, r0 - r2, i0 - i2
        cr, ci, dr, di = r1 + r3, i1 + i3, r1 - r3, i1 - i3
        out[a0] = ar + cr
        out[a0 + 8] = (br - di) * c1 - (bi + dr) * s1
        out[a0 + 16] = ((ar - cr) - (ai - ci)) * half
        out[a0 + 24] = (br + di) * s1 - (bi - dr) * c1
    return out


def owner_plane(ctx):
    z, y, core = ctx // 8, (ctx // 2) % 4, ctx % 2
    return 2 * ((z + y) % 2) + core


def owner_slot(ctx):
    z, y = ctx // 8, (ctx // 2) % 4
    return 2 * z + y // 2


def channel_block(ctx):
    return owner_plane(ctx) * 8 + owner_slot(ctx)


def summing_level(plane):
    return 2 * (plane % 2) + (1 - plane // 2)


def split(value):
    high = value.astype(BF16)
    return high, (value - high.astype(F32)).astype(BF16)


def times_table(table, kind, k1, re, im):
    wide = jnp.concatenate([re, im], axis=1)
    high, low = split(wide)

    def paired(part):
        other = jnp.concatenate([part[:, LANES:], -part[:, :LANES]], axis=1)
        return jnp.concatenate([part, other], axis=0)

    high, low = paired(high), paired(low)
    t_high, t_low = table[kind, k1], table[kind + 1, k1]
    dot = functools.partial(jnp.dot, preferred_element_type=F32)
    return dot(t_high, high) + dot(t_low, high) + dot(t_high, low)


def body(
    q_hbm, k_hbm, v_hbm, g_hbm, filt_hbm, tab_hbm,
    qg_hbm, got_back, lag_hbm, own_hbm, total_ref,
    q_in, k_in, v_in, g_in, filt_part, tab,
    send_m, send_g, send_b, got_m, got_k, got_g, work, spec_k, spec_m, spec_g,
    got_conv, parts, summed, lag,
    tile_mine, tile_x, tile_row, tile_all,
    load_sem, out_sem, ksend, krecv, kxsend, kxrecv, msend, mrecv, gsend, grecv,
    csend, crecv, bsend, brecv, psend, precv, lsend, lrecv, xsend, xrecv, asend, arecv, own_sem,
):
    d = lax.axis_index("dp")
    c = lax.axis_index("ctx")
    plane = owner_plane(c)
    slot = owner_slot(c)
    mine = channel_block(c)
    z, y = c // 8, (c // 2) % 4

    loads = {}
    def load(name, index, source, target):
        loads[name] = pltpu.make_async_copy(source, target, load_sem.at[index])
        loads[name].start()

    load("filt", 0, filt_hbm.at[pl.ds(pl.multiple_of(d * 32, 32), 32)], filt_part)
    load("k", 1, k_hbm.at[0], k_in)
    load("v", 2, v_hbm.at[0], v_in)

    level = (z + y) % 4
    helper = 2 * (1 - level % 2) + level // 2

    def lag_source(h):
        hz = h // 2
        hy = 2 * (h % 2) + (d // 2 + hz) % 2
        return hz * 8 + hy * 2 + d % 2

    def lag_target(i, of_plane):
        tz = i // 2
        ty = (summing_level(of_plane) - tz + 4) % 4
        return tz * 8 + ty * 2 + i % 2

    barrier = pltpu.get_barrier_semaphore()

    def greet(i, carry):
        pl.semaphore_signal(barrier, inc=1, device_id=(d, (c + i) % CTX), device_id_type=MESH)
        return carry

    lax.fori_loop(1, CTX, greet, 0)
    for step in range(1, DP):
        pl.semaphore_signal(barrier, inc=1, device_id=((d + step) % DP, c), device_id_type=MESH)

    def greet_lag(h, carry):
        pl.semaphore_signal(barrier, inc=1, device_id=(helper, lag_source(h)), device_id_type=MESH)
        return carry

    lax.fori_loop(0, 8, greet_lag, 0)
    pl.semaphore_wait(barrier, 31 + 3 + 8)

    def some_peers(action, step, first, last):
        core = lax.rem(c + step, 2)
        for dz, dy in STEPS[first:last]:
            action(lax.rem(z + dz, 4) * 8 + lax.rem(y + dy, 4) * 2 + core)

    def sibling(action):
        action(c + 1 - 2 * lax.rem(c, 2))

    def each_peer(action):
        def of_core(step, carry):
            some_peers(action, step, 0, len(STEPS))
            return carry

        lax.fori_loop(0, 2, of_core, 0)
        sibling(action)

    def wait_bytes(ref, sem):
        pltpu.make_async_copy(ref, ref, sem).wait()

    quarter = pl.ds(pl.multiple_of(d * 32, 32), 32)

    def filt_cols(block):
        return filt_part.at[:, pl.ds(pl.multiple_of(block * LANES, LANES), LANES)]

    loads["filt"].wait()

    def send_filter(t):
        pltpu.make_async_remote_copy(
            src_ref=filt_cols(channel_block(t)), dst_ref=got_k.at[c, quarter],
            send_sem=ksend, recv_sem=krecv, device_id=(d, t), device_id_type=MESH,
        ).start()

    each_peer(send_filter)
    own_copy = pltpu.make_async_copy(filt_cols(mine), got_k.at[c, quarter], own_sem)
    own_copy.start()

    def product(left, right, b):
        cols = pl.ds(pl.multiple_of(b * LANES, LANES), LANES)
        return left[:, cols].astype(F32) * right[:, cols].astype(F32)

    def send_block(t, store, target, ssem, rsem):
        pltpu.make_async_remote_copy(
            src_ref=store.at[channel_block(t)], dst_ref=target.at[c],
            send_sem=ssem, recv_sem=rsem, device_id=(d, t), device_id_type=MESH,
        ).start()

    loads["k"].wait()
    loads["v"].wait()
    load("g", 3, g_hbm.at[0], g_in)
    load("q", 4, q_hbm.at[0], q_in)

    def mixed(b, carry):
        send_m[b] = product(k_in, v_in, b)
        return carry

    lax.fori_loop(0, CTX, mixed, 0)
    got_m[c] = send_m[mine]

    blocks = pl.ds(0, CTX - 1)
    each_peer(lambda t: send_block(t, send_m, got_m, msend, mrecv))

    load("tab", 5, tab_hbm, tab)
    load("own", 6, filt_hbm.at[:, pl.ds(pl.multiple_of(d * 1024, 1024), 1024)], own_hbm)

    loads["g"].wait()
    loads["q"].wait()

    def gated(b, carry):
        send_g[b] = product(g_in, q_in, b)
        return carry

    lax.fori_loop(0, CTX, gated, 0)
    got_g[c] = send_g[mine]

    own_copy.wait()
    wait_bytes(got_k.at[pl.ds(0, 31), quarter], krecv)
    share = []
    for step in (1, 3, 2):
        copy = pltpu.make_async_remote_copy(
            src_ref=got_k.at[:, quarter], dst_ref=got_k.at[:, quarter],
            send_sem=kxsend.at[step - 1], recv_sem=kxrecv.at[step - 1],
            device_id=((d + step) % DP, c), device_id_type=MESH,
        )
        copy.start()
        share.append(copy)

    wait_bytes(send_m.at[blocks], msend)
    each_peer(lambda t: send_block(t, send_g, got_g, gsend, grecv))

    def forward(got, spec, scale=None):
        def lead(i, carry):
            rows = pl.ds(pl.multiple_of(i * 8, 8), 8)
            x = [got[a, rows] for a in range(CTX)]
            if scale is not None:
                x = [value * scale for value in x]
            for k1, (re, im) in enumerate(lead_forward(x)):
                work[k1, rows, :LANES] = re
                work[k1, rows, LANES:] = im
            return carry

        lax.fori_loop(0, ROWS // 8, lead, 0)

        def rest(i, carry):
            for k1 in (2 * i, 2 * i + 1):
                spec[k1] = times_table(tab, 0, k1, work[k1, :, :LANES], work[k1, :, LANES:])
            return carry

        lax.fori_loop(0, CTX // 2, rest, 0)

    def inverse(left, right, conjugate, out):
        def rest(i, carry):
            for k1 in (2 * i, 2 * i + 1):
                lr, li = left[k1, :, :LANES], left[k1, :, LANES:]
                rr, ri = right[k1, :, :LANES], right[k1, :, LANES:]
                if conjugate:
                    re, im = lr * rr + li * ri, li * rr - lr * ri
                else:
                    re, im = lr * rr - li * ri, -(lr * ri + li * rr)
                work[k1] = times_table(tab, 2, k1, re, im)
            return carry

        lax.fori_loop(0, CTX // 2, rest, 0)

        def lead(i, carry):
            rows = pl.ds(pl.multiple_of(i * 8, 8), 8)
            v = [(work[k1, rows, :LANES], -work[k1, rows, LANES:]) for k1 in range(CTX)]
            for a, value in enumerate(lead_inverse(v)):
                out[a, rows] = value
            return carry

        lax.fori_loop(0, ROWS // 8, lead, 0)

    def result_block(source, target, ssem, rsem):
        def send(t):
            pltpu.make_async_remote_copy(
                src_ref=source.at[t], dst_ref=target.at[mine],
                send_sem=ssem, recv_sem=rsem, device_id=(d, t), device_id_type=MESH,
            ).start()

        return send

    def keep_own(source, target):
        copy = pltpu.make_async_copy(source.at[c], target.at[mine], own_sem)
        copy.start()
        return copy

    loads["tab"].wait()
    wait_bytes(got_m.at[blocks], mrecv)
    forward(got_m, spec_m)
    for copy in share:
        copy.wait()
    forward(got_k, spec_k, PERIOD**-0.5)
    inverse(spec_k, spec_m, False, send_m)
    wait_bytes(send_g.at[blocks], gsend)
    each_peer(result_block(send_m, got_conv, csend, crecv))
    conv_own = keep_own(send_m, got_conv)

    wait_bytes(got_g.at[blocks], grecv)
    forward(got_g, spec_g)
    inverse(spec_m, spec_g, True, send_g)

    share = []
    for step in (1, 3, 2):
        to = (d + step) % DP
        for pair in range(4):
            copy = pltpu.make_async_remote_copy(
                src_ref=send_g.at[pl.ds(lag_target(2 * pair, to), 2)],
                dst_ref=parts.at[step - 1, pl.ds(2 * pair, 2)],
                send_sem=psend.at[step - 1, pair], recv_sem=precv.at[step - 1, pair],
                device_id=(to, c), device_id_type=MESH,
            )
            copy.start()
            share.append(copy)

    inverse(spec_k, spec_g, True, send_b)
    conv_own.wait()
    wait_bytes(send_m.at[blocks], csend)
    back_block = result_block(send_b, got_back, bsend, brecv)
    some_peers(back_block, 0, 0, 15)

    wait_bytes(got_conv.at[blocks], crecv)

    def finish_conv(b, carry):
        cols = pl.ds(pl.multiple_of(b * LANES, LANES), LANES)
        q_in[:, cols] = (g_in[:, cols].astype(F32) * got_conv[b]).astype(BF16)
        return carry

    lax.fori_loop(0, CTX, finish_conv, 0)
    query_out = pltpu.make_async_copy(q_in, qg_hbm, out_sem.at[0])
    query_out.start()

    for copy in share:
        copy.wait()

    def add_up(i, carry):
        squares, bad = carry
        value = (send_g[lag_target(i, d)] + parts[0, i]) + (parts[1, i] + parts[2, i])
        summed[i] = value
        value = value.reshape(16, 8, LANES)
        finite = jnp.abs(value) < jnp.inf
        return (
            squares + jnp.sum(value * value, axis=0),
            bad + jnp.sum(jnp.where(finite, 0.0, 1.0), axis=0),
        )

    nothing = jnp.zeros((8, LANES), F32)
    squares, bad = lax.fori_loop(0, 8, add_up, (nothing, nothing))
    tile_mine[:8] = squares
    tile_mine[8:] = bad
    share = []
    for step in range(1, DP):
        copy = pltpu.make_async_remote_copy(
            src_ref=tile_mine, dst_ref=tile_x.at[step - 1],
            send_sem=xsend.at[step - 1], recv_sem=xrecv.at[step - 1],
            device_id=((d + step) % DP, c), device_id_type=MESH,
        )
        copy.start()
        share.append(copy)

    def send_lag(i, carry):
        pltpu.make_async_remote_copy(
            src_ref=summed.at[i], dst_ref=lag.at[slot],
            send_sem=lsend, recv_sem=lrecv, device_id=(plane, lag_target(i, d)), device_id_type=MESH,
        ).start()
        return carry

    lax.fori_loop(0, 8, send_lag, 0)
    some_peers(back_block, 1, 0, BACK_EARLY)
    for copy in share:
        copy.wait()
    tile_row[...] = (tile_mine[...] + tile_x[0]) + (tile_x[1] + tile_x[2])

    def spread(t):
        pltpu.make_async_remote_copy(
            src_ref=tile_row, dst_ref=tile_all.at[c],
            send_sem=asend, recv_sem=arecv, device_id=(d, t), device_id_type=MESH,
        ).start()

    each_peer(spread)
    tile_all[c] = tile_row[...]
    some_peers(back_block, 1, BACK_EARLY, 15)
    sibling(back_block)
    back_own = keep_own(send_b, got_back)
    wait_bytes(lag, lrecv)

    lag_out = pltpu.make_async_copy(lag, lag_hbm, out_sem.at[1])
    lag_out.start()
    wait_bytes(tile_all.at[blocks], arecv)
    total_ref[...] = jnp.sum(tile_all[...], axis=0)
    back_own.wait()
    wait_bytes(got_back.at[blocks], brecv)

    wait_bytes(got_k.at[blocks, quarter], ksend)
    wait_bytes(send_b.at[blocks], bsend)
    wait_bytes(summed, lsend)
    wait_bytes(tile_all.at[blocks], asend)
    query_out.wait()
    lag_out.wait()
    loads["own"].wait()


def finish(
    query_ref, back_ref, lag_ref, total_ref, k_ref, v_ref, filt_ref, m1_ref, m2_ref,
    query_hbm, key_hbm, value_hbm, nf_hbm, n1_hbm, n2_hbm,
    keys, values, weight, first, second, out_sem,
):
    parts = keys.shape[0]
    width = keys.shape[2]
    per = width // LANES
    outs = []

    def store(source, target, index):
        copy = pltpu.make_async_copy(source, target, out_sem.at[index])
        copy.start()
        outs.append(copy)

    store(query_ref, query_hbm.at[0], 0)
    for part in range(parts):

        def gradients(i, carry):
            cols = pl.ds(pl.multiple_of(i * LANES, LANES), LANES)
            wide_cols = pl.ds(pl.multiple_of(part * width + i * LANES, LANES), LANES)
            value = back_ref[part * per + i]
            keys[part, :, cols] = (value * v_ref[0, :, wide_cols].astype(F32)).astype(BF16)
            values[part, :, cols] = (value * k_ref[0, :, wide_cols].astype(F32)).astype(BF16)
            return carry

        lax.fori_loop(0, per, gradients, 0)
        cols = pl.ds(part * width, width)
        store(keys.at[part], key_hbm.at[0, :, cols], 2 * part + 1)
        store(values.at[part], value_hbm.at[0, :, cols], 2 * part + 2)

    total_sq = jnp.sum(total_ref[:8])
    bad_count = jnp.sum(total_ref[8:])
    mean_sq = jnp.full((8, LANES), total_sq) * (1.0 / (PERIOD * 4096)) + 1e-06
    factor = jnp.minimum(1.0, 1.0 / jnp.sqrt(mean_sq))[:1]
    commit = (jnp.full((8, LANES), bad_count) == 0.0)[:1]

    def step(h, carry):
        cols = pl.ds(pl.multiple_of(h * LANES, LANES), LANES)
        clipped = lag_ref[h] * factor
        m1, m2, filt = m1_ref[:, cols], m2_ref[:, cols], filt_ref[:, cols]
        first_next = beta_first * m1 + (1.0 - beta_first) * clipped
        second_next = beta_second * m2 + (1.0 - beta_second) * clipped * clipped
        update = (
            first_next / correct_first / (jnp.sqrt(second_next / correct_second) + adam_epsilon)
            + decay_rate * filt
        )
        weight[:, cols] = jnp.where(commit, filt - learn_rate * update, filt)
        first[:, cols] = jnp.where(commit, first_next, m1)
        second[:, cols] = jnp.where(commit, second_next, m2)
        return carry

    lax.fori_loop(0, 8, step, 0)
    store(weight, nf_hbm, 2 * parts + 1)
    store(first, n1_hbm, 2 * parts + 2)
    store(second, n2_hbm, 2 * parts + 3)
    for copy in outs:
        copy.wait()


def on_device(query_act, key_act, value_act, out_grad, filter_weight, first_moment, second_moment):
    table = jnp.asarray(dft_tables())
    block = (CTX, ROWS, LANES)
    wide = (CTX, ROWS, 2 * LANES)
    vmem = pltpu.VMEM
    dma = pltpu.SemaphoreType.DMA
    anywhere = pl.BlockSpec(memory_space=pltpu.HBM)
    either = pl.BlockSpec(memory_space=pl.ANY)
    stream = jax.ShapeDtypeStruct(query_act.shape, BF16)
    state = jax.ShapeDtypeStruct(first_moment.shape, F32)
    query_grad, back_in, lag_grad, own_filter, total = pl.pallas_call(
        body,
        out_shape=(
            jax.ShapeDtypeStruct((ROWS, 4096), BF16),
            jax.ShapeDtypeStruct(block, F32),
            jax.ShapeDtypeStruct((8, ROWS, LANES), F32),
            state,
            jax.ShapeDtypeStruct((16, LANES), F32),
        ),
        in_specs=[anywhere] * 6,
        out_specs=(either, either, either, either, pl.BlockSpec(memory_space=pltpu.VMEM)),
        scratch_shapes=[
            vmem((ROWS, 4096), BF16), vmem((ROWS, 4096), BF16),
            vmem((ROWS, 4096), BF16), vmem((ROWS, 4096), BF16),
            vmem((32, 4096), F32),
            vmem((4,) + wide, BF16),
            vmem(block, F32), vmem(block, F32), vmem(block, F32),
            vmem(block, F32), vmem(block, F32), vmem(block, F32),
            vmem(wide, F32), vmem(wide, F32), vmem(wide, F32), vmem(wide, F32),
            vmem(block, F32),
            vmem((3, 8, ROWS, LANES), F32), vmem((8, ROWS, LANES), F32), vmem((8, ROWS, LANES), F32),
            vmem((16, LANES), F32), vmem((3, 16, LANES), F32), vmem((16, LANES), F32),
            vmem((CTX, 16, LANES), F32),
            dma((7,)), dma((2,)), dma, dma, dma((3,)), dma((3,)), dma, dma, dma, dma,
            dma, dma, dma, dma, dma((3, 4)), dma((3, 4)), dma, dma, dma((3,)), dma((3,)), dma, dma, dma,
        ],
        compiler_params=pltpu.CompilerParams(
            collective_id=0, has_side_effects=True, vmem_limit_bytes=VMEM_MIB * 2**20
        ),
    )(query_act, key_act, value_act, out_grad, filter_weight, table)
    cuts = 4
    local = pl.BlockSpec(memory_space=pltpu.VMEM)
    return pl.pallas_call(
        finish,
        out_shape=(stream, stream, stream, state, state, state),
        in_specs=[local] * 9,
        out_specs=(anywhere,) * 6,
        scratch_shapes=[
            vmem((cuts, ROWS, 4096 // cuts), BF16), vmem((cuts, ROWS, 4096 // cuts), BF16),
            vmem((ROWS, 1024), F32), vmem((ROWS, 1024), F32), vmem((ROWS, 1024), F32),
            dma((2 * cuts + 4,)),
        ],
        compiler_params=pltpu.CompilerParams(vmem_limit_bytes=16 * 2**20),
    )(query_grad, back_in, lag_grad, total, key_act, value_act, own_filter, first_moment, second_moment)


def solution(mesh):
    return jax.shard_map(
        on_device,
        mesh=mesh,
        in_specs=(
            P("dp", "ctx", None),
            P("dp", "ctx", None),
            P("dp", "ctx", None),
            P("dp", "ctx", None),
            P("ctx", None),
            P("ctx", "dp"),
            P("ctx", "dp"),
        ),
        out_specs=(
            P("dp", "ctx", None),
            P("dp", "ctx", None),
            P("dp", "ctx", None),
            P("ctx", "dp"),
            P("ctx", "dp"),
            P("ctx", "dp"),
        ),
        check_vma=False,
    )
```
